256 devices in a mesh: dp: 8 (over z_hi, y), expert: 8 (over z_lo, core), tensor: 4 (over x).
Axes of the slice: x: 4, y: 4, z: 8 (z_hi: 2, z_lo: 4; z = z_hi * 4 + z_lo), core: 2. Of those that a mesh axis runs over, the one named last changes fastest.
Arguments:
- tokens: bfloat16 [1024, 6144], P(('dp', 'expert', 'tensor')), may hold values from -6 to 6
- out_grad: bfloat16 [1024, 6144], P(('dp', 'expert', 'tensor')), may hold values from -6 to 6
- routes: int32 [1024, 2], P(('dp', 'expert', 'tensor')), may hold values from 0 to 7, all different within a row; in each aligned block of 4 rows (0 to 3, 4 to 7, ...) at most 2 rows name the same one
- tasks: int32 [1024], P(('dp', 'expert', 'tensor')), may hold values from 0 to 3
- route_probs: float32 [1024, 2], P(('dp', 'expert', 'tensor')), may hold values from 0.2 to 1
- gate_matrix_frozen: bfloat16 [8, 6144, 8192], P('expert', None, ('dp', 'tensor')), may hold values from -0.078125 to 0.078125
- w_up: bfloat16 [8, 6144, 8192], P('expert', None, ('dp', 'tensor')), may hold values from -0.078125 to 0.078125
- down_matrix: bfloat16 [8, 8192, 6144], P('expert', ('dp', 'tensor')), may hold values from -0.0625 to 0.0625
- gate_down: bfloat16 [8, 6144, 64], P('expert'), may hold values from -0.078125 to 0.078125
- gate_adapter_right: bfloat16 [8, 64, 8192], P('expert', None, ('dp', 'tensor')), may hold values from -1.5 to 1.5
- down_adapter_left: bfloat16 [8, 8192, 64], P('expert', ('dp', 'tensor')), may hold values from -0.0625 to 0.0625
- down_adapter_right: bfloat16 [8, 64, 6144], P('expert'), may hold values from -1.5 to 1.5
Outputs:
- mixed: bfloat16 [1024, 6144], P(('dp', 'expert', 'tensor'))
- grad_gate_down: bfloat16 [8, 6144, 64], P('expert')
- grad_gate_lift: bfloat16 [8, 64, 8192], P('expert', None, ('dp', 'tensor'))
- grad_down_down: bfloat16 [8, 8192, 64], P('expert', ('dp', 'tensor'))
- grad_down_lift: bfloat16 [8, 64, 6144], P('expert')
The draws below stay inside these ranges and needn't reach their ends.
Inputs may be any that keep to these rules, and one draw needn't show every extreme that they name: `routes`: within the rows of one device no expert is named by more than 2 rows.
All inputs are finite; a program needn't handle non-finite values.
Results may differ from the reference program's by a relative error of at most 0.0066.
Values may be sent and summed in bfloat16 or wider, within the bound.
A program may use at most 128 MiB of HBM per device.

```python
import math
import jax
import jax.numpy as jnp
import numpy as np
from jax import lax

D = 6144
FF = 8192
RANK = 16
NTASK = 4
TOK_DEV = 4
EXPERTS = 8
CAP = 2
NR = 64
TOKENS = 1024
DEVICES = 256


def plant(entries, stream_key, smallest, high):
    dims = entries.shape
    spot = [jax.random.randint(jax.random.fold_in(stream_key, axis), (), 0, dims[axis]) for axis in range(len(dims))]
    entries = entries.at[tuple(spot)].set(smallest)
    longest = dims.index(max(dims))
    spot[longest] = (spot[longest] + 1) % dims[longest]
    return entries.at[tuple(spot)].set(high)


def shard_levels(key, extent, split, smallest, largest):
    gain = 1.0
    for position, parts in split:
        steps = jax.random.uniform(jax.random.fold_in(jax.random.fold_in(key, 6), position), (parts,), jnp.float32, smallest / len(split), largest / len(split))
        gain = gain * jnp.repeat(jnp.exp(steps), extent[position] // parts).reshape((-1,) + (1,) * (len(extent) - 1 - position))
    return gain


def shared_out(rng, own, number, rows, amount, top, most, lean):
    order = jax.random.permutation(rng, amount)
    heavy_load, common = load_shares(amount, rows * top, most, lean, True), load_shares(amount, rows * top, most, lean, False)
    places = jnp.arange(amount)

    def named(sizes, turn):
        used = int((sizes > 0).sum())
        fixed = max(1, used // 4)
        moved = fixed + (places - fixed + turn * (used - fixed)) % max(1, amount - fixed)
        return jnp.zeros((amount,), jnp.int32).at[order[jnp.where(places < fixed, places, moved)]].set(jnp.asarray(sizes, jnp.int32))

    sizes = jnp.where(number % 4 == 0, named(heavy_load, number // 4), named(common, number - number // 4 - 1))
    mixed = jax.random.permutation(jax.random.fold_in(own, 3), amount)
    source_of, sink = mixed[0:amount // 2 * 2:2], mixed[1:amount // 2 * 2:2]
    margin = jnp.minimum(sizes[source_of] - 1, most - sizes[sink]) // 2
    margin = jnp.where((source_of == order[0]) | (sink == order[0]) | (sizes[sink] == 0), 0, jnp.maximum(margin, 0))
    moved = jax.random.randint(jax.random.fold_in(own, 4), (amount // 2,), 0, 1 << 20) % (margin + 1)
    sizes = sizes.at[source_of].add(-moved).at[sink].add(moved)
    labels = jnp.searchsorted(jnp.cumsum(sizes), jnp.arange(rows * top), side="right").astype(jnp.int32)
    table = labels.reshape(top, rows).T
    table = table[jax.random.permutation(jax.random.fold_in(own, 1), rows)]
    turn = jax.random.randint(jax.random.fold_in(own, 2), (rows, 1), 0, top)
    return jnp.take_along_axis(table, (jnp.arange(top)[None, :] + turn) % top, axis=1)


def load_shares(count, total, reach, lean, full):
    weights = [(1 << 20) // math.isqrt(rank ** lean) + 1 for rank in range(1, count + 1)]
    largest = reach if full else min(reach, max(-(-total // count), total * weights[0] // sum(weights)))
    least = 1 if total - largest >= count - 1 else 0
    holding, surplus = [largest] + [least] * (count - 1), total - largest - least * (count - 1)
    while surplus > 0:
        free = [i for i in range(1, count) if holding[i] < largest] or [i for i in range(1, count) if holding[i] < reach]
        pool, remaining = sum([weights[i] for i in free]), surplus
        for i in free:
            extra = min(reach - holding[i], max(1, remaining * weights[i] // pool), surplus)
            holding[i] = holding[i] + extra
            surplus = surplus - extra
    return np.array(holding)


def scatter_about(own_key, shape, width, bound, pieces=(), kind=jnp.bfloat16):
    drawn = jax.random.normal(own_key, shape, jnp.float32) * width
    if len(pieces) > 0:
        drawn = shard_levels(own_key, shape, pieces, -0.22, 0.18) * drawn
    return jnp.clip(drawn, min=-bound, max=bound).astype(kind)


def setup_inputs(seed: int = 0) -> dict:
    streams_of = jax.random.split(jax.random.key(seed), 13)
    tokens = scatter_about(streams_of[0], (TOKENS, D), 1.0, 6.0, ((0, 256),))
    out_grad = scatter_about(streams_of[1], (TOKENS, D), 1.0, 6.0, ((0, 256),))
    routes_keys = jax.random.split(jax.random.fold_in(streams_of[2], 1), TOKENS // TOK_DEV)
    routes_turns = jax.random.permutation(jax.random.fold_in(streams_of[2], 3), TOKENS // TOK_DEV)
    routes = jax.vmap(lambda own, number: shared_out(jax.random.fold_in(streams_of[2], 2), own, number, TOK_DEV, EXPERTS, 2, CAP, 2))(routes_keys, routes_turns).reshape((TOKENS, 2))
    tasks = plant(jax.random.randint(streams_of[3], (TOKENS,), 0, NTASK), jax.random.fold_in(streams_of[3], 1), 0, NTASK - 1).astype(jnp.int32)
    route_probs = jnp.clip(0.2 + 0.8 * jax.random.uniform(streams_of[4], (TOKENS, 2), jnp.float32) ** shard_levels(streams_of[4], (TOKENS, 2), ((0, 256),), -0.2, 0.2), 0.2, 1.0)
    gate_matrix_frozen = scatter_about(streams_of[5], (EXPERTS, D, FF), D ** -0.5, 0.078125, ((0, 8), (2, 32)))
    w_up = scatter_about(streams_of[6], (EXPERTS, D, FF), D ** -0.5, 0.078125, ((0, 8), (2, 32)))
    down_matrix = scatter_about(streams_of[7], (EXPERTS, FF, D), FF ** -0.5, 0.0625, ((0, 8), (1, 32)))
    gate_down = scatter_about(streams_of[8], (EXPERTS, D, NR), D ** -0.5, 0.078125, ((0, 8),))
    gate_adapter_right = scatter_about(streams_of[9], (EXPERTS, NR, FF), RANK ** -0.5, 1.5, ((0, 8), (2, 32)))
    down_adapter_left = scatter_about(streams_of[10], (EXPERTS, FF, NR), FF ** -0.5, 0.0625, ((0, 8), (1, 32)))
    down_adapter_right = scatter_about(streams_of[11], (EXPERTS, NR, D), RANK ** -0.5, 1.5, ((0, 8),))
    return {"tokens": tokens, "out_grad": out_grad, "routes": routes, "tasks": tasks, "route_probs": route_probs, "gate_matrix_frozen": gate_matrix_frozen, "w_up": w_up, "down_matrix": down_matrix, "gate_down": gate_down, "gate_adapter_right": gate_adapter_right, "down_adapter_left": down_adapter_left, "down_adapter_right": down_adapter_right}


adapter_scale = 0.5


def matrix_multiply(left, right):
    return jnp.dot(left.astype(jnp.float32), right.astype(jnp.float32), precision=lax.Precision.HIGHEST)


def reference(tokens, out_grad, routes, tasks, route_probs, gate_matrix_frozen, w_up, down_matrix, gate_down, gate_adapter_right, down_adapter_left, down_adapter_right):
    flat_expert = routes.reshape(-1).astype(jnp.int32)
    flat_token = jnp.arange(flat_expert.shape[0], dtype=jnp.int32) // 2
    flat_prob = route_probs.reshape(-1)
    limit = CAP * DEVICES
    bands = jnp.arange(NTASK * RANK, dtype=jnp.int32) // RANK
    mixed = jnp.zeros((TOKENS, D), jnp.float32)
    left_gradients_one, right_gradients_one, left_gradients_two, right_gradients_two = [], [], [], []
    for expert_index in range(EXPERTS):
        member = flat_expert == expert_index
        chosen = jnp.nonzero(member, size=limit, fill_value=0)[0].astype(jnp.int32)
        count = jnp.sum(member.astype(jnp.int32))
        valid = jnp.arange(limit, dtype=jnp.int32) < count
        token_ids = flat_token[chosen]
        input_rows = jnp.where(valid[:, None], tokens[token_ids], jnp.zeros((), tokens.dtype))
        probs = jnp.where(valid, flat_prob[chosen], jnp.zeros((), flat_prob.dtype))
        mask = tasks[token_ids].astype(jnp.int32)[:, None] == bands[None, :]
        gate_lowrank = jnp.where(mask, matrix_multiply(input_rows, gate_down[expert_index]), 0.0).astype(jnp.bfloat16)
        gate_activation = matrix_multiply(input_rows, gate_matrix_frozen[expert_index]) + adapter_scale * matrix_multiply(gate_lowrank, gate_adapter_right[expert_index])
        upval = matrix_multiply(input_rows, w_up[expert_index])
        hidden_state = (jax.nn.silu(gate_activation) * upval).astype(jnp.bfloat16)
        latent_lowrank = jnp.where(mask, matrix_multiply(hidden_state, down_adapter_left[expert_index]), 0.0).astype(jnp.bfloat16)
        block_output = matrix_multiply(hidden_state, down_matrix[expert_index]) + adapter_scale * matrix_multiply(latent_lowrank, down_adapter_right[expert_index])
        mixed = mixed.at[token_ids].add(probs[:, None] * block_output)
        output_gradient = (probs[:, None] * out_grad[token_ids].astype(jnp.float32)).astype(jnp.bfloat16)
        combined_lowrank = jnp.where(mask, matrix_multiply(output_gradient, down_adapter_right[expert_index].T), 0.0).astype(jnp.bfloat16)
        hidden_gradient = matrix_multiply(output_gradient, down_matrix[expert_index].T) + adapter_scale * matrix_multiply(combined_lowrank, down_adapter_left[expert_index].T)
        sig = jax.nn.sigmoid(gate_activation)
        gate_gradient = (hidden_gradient * upval * sig * (1.0 + gate_activation * (1.0 - sig))).astype(jnp.bfloat16)
        expert_lowrank = jnp.where(mask, matrix_multiply(gate_gradient, gate_adapter_right[expert_index].T), 0.0)
        left_gradients_one.append((adapter_scale * matrix_multiply(input_rows.T, expert_lowrank)).astype(jnp.bfloat16))
        right_gradients_one.append((adapter_scale * matrix_multiply(gate_lowrank.T, gate_gradient)).astype(jnp.bfloat16))
        left_gradients_two.append((adapter_scale * matrix_multiply(hidden_state.T, combined_lowrank)).astype(jnp.bfloat16))
        right_gradients_two.append((adapter_scale * matrix_multiply(latent_lowrank.T, output_gradient)).astype(jnp.bfloat16))
    return (mixed.astype(jnp.bfloat16), jnp.stack(left_gradients_one), jnp.stack(right_gradients_one), jnp.stack(left_gradients_two), jnp.stack(right_gradients_two))
```

```python
import functools

import jax
import jax.numpy as jnp
from jax import lax
from jax.experimental import pallas as pl
from jax.experimental.pallas import tpu as pltpu
from jax.sharding import PartitionSpec as P

RANK = 16
SCALE = 0.5
MESH = pl.DeviceIdType.MESH
BF = jnp.bfloat16
F32 = jnp.float32
WIDTH = 512
TILE = 256
MAX_COPIES = 400

RS_PHASES = (
    (("x", 4, (4, 8, 16, 512), (2, 8, 16, 512)), ("y", 4, (8, 16, 512), (4, 16, 512)), ("z", 8, (16, 512), None)),
    (("y", 4, (4, 8, 16, 512), (2, 8, 16, 512)), ("z", 8, (4, 16, 512), (2, 16, 512)), ("x", 4, (16, 512), None)),
    (("z", 8, (4, 4, 16, 512), (2, 4, 16, 512)), ("x", 4, (4, 16, 512), (2, 16, 512)), ("y", 4, (16, 512), None)),
)


def rs_buffers():
    shapes = {}
    for k, phases in enumerate(RS_PHASES):
        for p, (_, n, block, half) in enumerate(phases):
            for way in range(2):
                for slot in range(n // 2):
                    shape = block
                    if slot == 0:
                        if half is None and way == 1:
                            continue
                        shape = half or block
                    shapes[("rs", k, p, way, slot)] = pltpu.VMEM(shape, BF)
    return shapes


def scratch():
    shapes = {
        "X": pltpu.VMEM((6, 4, 4, 8, 16, WIDTH), BF),
        "G": pltpu.VMEM((6, 4, 4, 8, 16, WIDTH), BF),
        "OUT": pltpu.VMEM((3, 4, 4, 8, 16, WIDTH), BF),
        "STAGE": pltpu.VMEM((3, 2, 4, 8, 16, WIDTH), BF),
        "SIB": pltpu.VMEM((3, 4, 4, 8, 16, WIDTH), BF),
        "DOWN": pltpu.VMEM((256, 6144), BF),
        "W": pltpu.VMEM((2, 2, WIDTH, 256), BF),
        "G1T": pltpu.VMEM((64, 6144), BF),
        "L2": pltpu.VMEM((64, 6144), BF),
        "ACC": pltpu.VMEM((1024, 512), F32),
        "A64": pltpu.VMEM((1024, 64), F32),
        "H": pltpu.VMEM((1024, 256), F32),
        "MK": pltpu.VMEM((1024, 128), F32),
        "PB": pltpu.VMEM((1024, 128), F32),
        "ZP": pltpu.VMEM((1024, 64), F32),
        "HID": pltpu.VMEM((1024, 256), BF),
        "DG": pltpu.VMEM((1024, 256), BF),
        "A": pltpu.VMEM((1024, 64), BF),
        "ZS": pltpu.VMEM((1024, 64), BF),
        "C": pltpu.VMEM((1024, 64), BF),
        "T32": pltpu.VMEM((2, 4, 4, 1536), F32),
        "M32": pltpu.VMEM((4, 128), F32),
        "R": pltpu.VMEM((2, 4, 4, 1536), F32),
        "MR": pltpu.VMEM((4, 4, 128), F32),
        "F": pltpu.VMEM((2, 16, 1536), F32),
        "FM": pltpu.VMEM((16, 128), F32),
        "MZ": pltpu.VMEM((8, 16, 128), BF),
        "MF": pltpu.VMEM((2, 4, 16, 128), BF),
        "ZR": pltpu.VMEM((4, 32, 256), F32),
        "AX": pltpu.VMEM((4, 32, 256), F32),
        "YS": pltpu.VMEM((4, 8, 256), F32),
        "AY": pltpu.VMEM((4, 8, 256), F32),
        "HS": pltpu.VMEM((8, 256), F32),
        "HR": pltpu.VMEM((8, 256), F32),
        "FY": pltpu.VMEM((4, 8, 256), F32),
        "FX": pltpu.VMEM((4, 4, 8, 256), F32),
        "LZ": pltpu.VMEM((64, 1024), BF),
        "LR": pltpu.VMEM((128, 1024), BF),
        "S32": pltpu.VMEM((4, 4, 1536), F32),
        "MX": pltpu.VMEM((4, 4, 1536), F32),
        "send": pltpu.SemaphoreType.DMA((MAX_COPIES,)),
        "recv": pltpu.SemaphoreType.DMA((MAX_COPIES,)),
        "local": pltpu.SemaphoreType.DMA((8,)),
    }
    shapes.update(rs_buffers())
    return shapes


def dot(a, b, ca=1, cb=0):
    return lax.dot_general(a, b, (((ca,), (cb,)), ((), ())), preferred_element_type=F32)


def body(names, tok, og, meta, wg, wu, down, g1t, l1, g2t, l2, mixed, o_gd, o_gl, o_dd, o_dl, *refs):
    s = dict(zip(names, refs))
    X, G, OUT, SIB = s["X"], s["G"], s["OUT"], s["SIB"]
    dp, ex, x = lax.axis_index("dp"), lax.axis_index("expert"), lax.axis_index("tensor")
    h, y = dp // 4, dp % 4
    zl, c = ex // 2, ex % 2
    z = h * 4 + zl
    xlo, xhi = x % 2, x // 2
    xp = xlo * 2 + xhi
    grp = xlo * 2 + c

    def device(x_, y_, z_, c_):
        return ((z_ // 4) * 4 + y_, (z_ % 4) * 2 + c_, x_)

    def around(v, d, n):
        return lax.rem(v + (d + n), n)

    def xperm(i):
        return lax.rem(i, 2) * 2 + i // 2

    xdev = [device(around(x, d, 4), y, z, c) for d in range(4)]
    ydev = [device(x, around(y, d, 4), z, c) for d in range(4)]
    zdev = {1: device(x, y, around(z, 1, 8), c), -1: device(x, y, around(z, -1, 8), c)}
    far = device(x, y, around(z, 4, 8), c)
    sibling = device(x, y, z, 1 - c)
    xpair = xhi * 2 + (1 - xlo)
    pair = device(xpair, y, z, c)
    pair_sibling = device(xpair, y, z, 1 - c)
    steps = {"x": (x, 4, xdev[1], xdev[3]), "y": (y, 4, ydev[1], ydev[3]), "z": (z, 8, zdev[1], zdev[-1])}

    count = [0]
    pending = []

    def send(src, dst, target):
        i = count[0]
        count[0] += 1
        copy = pltpu.make_async_remote_copy(
            src_ref=src, dst_ref=dst, send_sem=s["send"].at[i], recv_sem=s["recv"].at[i],
            device_id=target, device_id_type=MESH,
        )
        copy.start()
        pending.append(copy)
        return copy

    local_down = pltpu.make_async_copy(down, s["DOWN"], s["local"].at[0])
    local_g1 = pltpu.make_async_copy(g1t, s["G1T"], s["local"].at[1])
    local_l2 = pltpu.make_async_copy(l2, s["L2"], s["local"].at[2])

    def weight_copies(j):
        b = order_b[j]
        rows = pl.ds(pl.multiple_of(b * WIDTH, WIDTH), WIDTH)
        slot = j % 2
        return (
            pltpu.make_async_copy(wg.at[rows, :], s["W"].at[slot, 0], s["local"].at[3 + 2 * slot]),
            pltpu.make_async_copy(wu.at[rows, :], s["W"].at[slot, 1], s["local"].at[4 + 2 * slot]),
        )

    use = [(cc, k, lo) for k in (0, 1, 2) for cc in (0, 1) for lo in (0, 1)]
    half_of = (c, 1 - c)
    order_b = [lo * 6 + half_of[cc] * 3 + k for cc, k, lo in use]

    barrier = pltpu.get_barrier_semaphore()
    greeted = xdev[1:] + ydev[1:] + [zdev[1], zdev[-1], far, sibling, pair_sibling]
    for target in greeted:
        pl.semaphore_signal(barrier, inc=1, device_id=target, device_id_type=MESH)
    local_down.start()
    local_g1.start()
    local_l2.start()
    for j in (0, 1):
        for copy in weight_copies(j):
            copy.start()
    for q in range(4):
        s["T32"][0, q] = tok[:, q * 1536:(q + 1) * 1536].astype(F32)
        s["T32"][1, q] = og[:, q * 1536:(q + 1) * 1536].astype(F32)
    s["M32"][...] = meta[...].astype(F32)
    pl.semaphore_wait(barrier, len(greeted))

    mates = ((xlo * 2 + 1 - c, sibling), ((1 - xlo) * 2 + c, pair), ((1 - xlo) * 2 + 1 - c, pair_sibling))
    first = {}
    for a in range(2):
        first[a] = [send(s["T32"].at[a, g], s["R"].at[a, grp], d) for g, d in mates]
        if a == 0:
            first["m"] = [send(s["M32"], s["MR"].at[grp], d) for g, d in mates]
    s["R"][0, grp] = s["T32"][0, grp]
    s["R"][1, grp] = s["T32"][1, grp]
    s["MR"][grp] = s["M32"][...]

    def own_block(a, buf):
        for copy in first[a]:
            copy.wait_recv()
        for q in range(4):
            s["F"][a, q * 4:q * 4 + 4, :] = s["R"][a, q]
        for k in range(3):
            buf[c * 3 + k, xp, y, z] = s["F"][a, :, k * WIDTH:(k + 1) * WIDTH].astype(BF)

    def all_gather(n, me, plus, minus, blk, half, arrived):
        up, dn = send(blk(me), blk(me), plus), send(blk(me), blk(me), minus)
        arrived(blk(me))
        yield
        reach = n // 2
        for d in range(1, reach):
            last = d == reach - 1
            a, b = around(me, -d, n), around(me, d, n)
            up.wait_recv()
            if not last:
                up = send(blk(a), blk(a), plus)
            elif half is None:
                up = send(blk(a), blk(a), plus)
            else:
                up = send(half(a, 0), half(a, 0), plus)
            arrived(blk(a))
            dn.wait_recv()
            if not last:
                dn = send(blk(b), blk(b), minus)
            elif half is not None:
                dn = send(half(b, 1), half(b, 1), minus)
            arrived(blk(b))
            yield
        opposite = around(me, reach, n)
        up.wait_recv()
        if half is None:
            arrived(blk(opposite))
        else:
            arrived(half(opposite, 0))
            dn.wait_recv()
            arrived(half(opposite, 1))

    def gather_colour(k, buf, forwards):
        ck = c * 3 + k
        if k == 0:
            phases = (
                ("z", lambda i: buf.at[ck, xp, y, i], None),
                ("y", lambda i: buf.at[ck, xp, i], lambda i, g: buf.at[ck, xp, i, pl.ds(4 * g, 4)]),
                ("x", lambda i: buf.at[ck, xperm(i)], lambda i, g: buf.at[ck, xperm(i), pl.ds(2 * g, 2)]),
            )
        elif k == 1:
            phases = (
                ("x", lambda i: buf.at[ck, xperm(i), y, z], None),
                ("z", lambda i: buf.at[ck, :, y, i], lambda i, g: buf.at[ck, pl.ds(2 * g, 2), y, i]),
                ("y", lambda i: buf.at[ck, :, i], lambda i, g: buf.at[ck, pl.ds(2 * g, 2), i]),
            )
        else:
            phases = (
                ("y", lambda i: buf.at[ck, xp, i, z], None),
                ("x", lambda i: buf.at[ck, xperm(i), :, z], lambda i, g: buf.at[ck, xperm(i), pl.ds(2 * g, 2), z]),
                ("z", lambda i: buf.at[ck, :, :, i], lambda i, g: buf.at[ck, pl.ds(2 * g, 2), :, i]),
            )
        for p, (axis, blk, half) in enumerate(phases):
            me, n, plus, minus = steps[axis]
            if p == 2:
                arrived = lambda ref: forwards.append(send(ref, ref, sibling))
            else:
                arrived = lambda ref: None
            yield from all_gather(n, me, plus, minus, blk, half, arrived)

    def gather_meta():
        for copy in first["m"]:
            copy.wait_recv()
        for q in range(4):
            s["FM"][q * 4:q * 4 + 4, :] = s["MR"][q]
        s["MZ"][z] = pltpu.roll(s["FM"][...], z * 16, 1).astype(BF)
        yield from all_gather(8, z, zdev[1], zdev[-1], lambda i: s["MZ"].at[i], None, lambda ref: None)
        total = s["MZ"][0].astype(F32)
        for i in range(1, 8):
            total = total + s["MZ"][i].astype(F32)
        s["MF"][xhi, y] = total.astype(BF)
        yield from all_gather(4, y, ydev[1], ydev[3], lambda i: s["MF"].at[xhi, i], None, lambda ref: None)
        ref = s["MF"].at[xhi]
        plus, minus = send(ref, s["MF"].at[xhi], xdev[2]), None
        yield
        plus.wait_recv()

    def pump(gens, times=1):
        for _ in range(times):
            for gen in list(gens):
                try:
                    next(gen)
                except StopIteration:
                    gens.remove(gen)

    own_block(0, X)
    fx, fg = [], []
    xgens = [gather_colour(2, X, fx), gather_colour(1, X, fx), gather_colour(0, X, fx), gather_meta()]
    pump(xgens, 1)
    own_block(1, G)
    pump(xgens, 4)
    ggens = [gather_colour(2, G, fg), gather_colour(1, G, fg), gather_colour(0, G, fg)]
    while xgens:
        pump(xgens, 1)
        pump(ggens, 1)

    fields = s["MF"][...].astype(F32).reshape(128, 128)
    me_f = ex.astype(F32)
    band = (lax.broadcasted_iota(jnp.int32, (128, 64), 1) // RANK).astype(F32)
    for i in range(8):
        f = fields if i == 0 else pltpu.roll(fields, 128 - 16 * i, 1)
        hit0 = jnp.where(f[:, 0:1] == me_f, 1.0, 0.0)
        hit1 = jnp.where(f[:, 1:2] == me_f, 1.0, 0.0)
        p0 = f[:, 3:4] + f[:, 4:5] + f[:, 5:6]
        p1 = f[:, 6:7] + f[:, 7:8] + f[:, 8:9]
        p = hit0 * p0 + hit1 * p1
        mask = jnp.where(f[:, 2:3] == band, 1.0, 0.0) * (hit0 + hit1)
        both = jnp.concatenate([mask, mask * p], axis=1)
        wide = jnp.broadcast_to(p, (128, 128))
        for g in range(8):
            rows = slice((g * 8 + i) * 16, (g * 8 + i) * 16 + 16)
            s["MK"][rows, :] = both[g * 16:g * 16 + 16, :]
            s["PB"][rows, :] = wide[g * 16:g * 16 + 16, :]

    def rows_of(t):
        return pl.ds(pl.multiple_of(t * TILE, TILE), TILE)

    def tile(buf, ck, lo, t):
        return buf[ck, lo * 2 + t // 2, pl.ds((t % 2) * 2, 2)].reshape(TILE, WIDTH)

    for copy in fx:
        copy.wait_recv()
    local_g1.wait()

    for j, (cc, k, lo) in enumerate(use):
        ck = half_of[cc] * 3 + k
        cols = pl.ds(pl.multiple_of(order_b[j] * WIDTH, WIDTH), WIDTH)
        for copy in weight_copies(j):
            copy.wait()

        @pl.loop(0, 4)
        def _(t, ck=ck, lo=lo, cols=cols, j=j):
            rows = rows_of(t)
            xt = tile(X, ck, lo, t)
            ga = dot(xt, s["W"][j % 2, 0])
            up = dot(xt, s["W"][j % 2, 1])
            lr = dot(xt, s["G1T"][:, cols], 1, 1)
            if j == 0:
                s["ACC"][rows, 0:256] = ga
                s["ACC"][rows, 256:512] = up
                s["A64"][rows, :] = lr
            else:
                s["ACC"][rows, 0:256] += ga
                s["ACC"][rows, 256:512] += up
                s["A64"][rows, :] += lr

        if j + 2 < len(use):
            for copy in weight_copies(j + 2):
                copy.start()
        pump(ggens, 1)

    @pl.loop(0, 4)
    def _(t):
        rows = rows_of(t)
        mask = s["MK"][rows, 0:64]
        a = (s["A64"][rows, :] * mask).astype(BF)
        gate = s["ACC"][rows, 0:256] + SCALE * dot(a, l1[...])
        s["ACC"][rows, 0:256] = gate
        s["A"][rows, :] = a
        hid = (gate * jax.nn.sigmoid(gate) * s["ACC"][rows, 256:512]).astype(BF)
        s["HID"][rows, :] = hid
        zp = dot(hid, g2t[...], 1, 1) * mask
        s["ZP"][rows, :] = zp
        s["ZS"][rows, :] = (SCALE * zp).astype(BF)

    local_down.wait()
    local_l2.wait()
    pump(ggens, 1)

    def out_block(dst, cc, k, lo):
        b = lo * 6 + half_of[cc] * 3 + k
        cols = pl.ds(pl.multiple_of(b * WIDTH, WIDTH), WIDTH)

        @pl.loop(0, 4)
        def _(t):
            rows = rows_of(t)
            o = dot(s["HID"][rows, :], s["DOWN"][:, cols]) + dot(s["ZS"][rows, :], s["L2"][:, cols])
            p = s["PB"][rows, :]
            o = o * jnp.concatenate([p, p, p, p], axis=1)
            dst[t // 2, pl.ds((t % 2) * 2, 2)] = o.astype(BF).reshape(2, 8, 16, WIDTH)

    handed = []
    order_k = (2, 1, 0)
    for n, (k, lo) in enumerate([(k, lo) for k in order_k for lo in (0, 1)]):
        slot = s["STAGE"].at[n % 3]
        if n >= 3:
            handed[n - 3].wait_send()
            pending[:] = [copy for copy in pending if copy is not handed[n - 3]]
        out_block(slot, 1, k, lo)
        handed.append(send(slot, SIB.at[k, pl.ds(lo * 2, 2)], sibling))
        out_block(OUT.at[k, pl.ds(lo * 2, 2)], 0, k, lo)
        pump(ggens, 1)
    while ggens:
        pump(ggens, 1)

    def add_block(dst, src, shape):
        lead = shape[:-2]
        total = 1
        for v in lead:
            total *= v
        if total == 1:
            dst[...] = (dst[...].astype(F32) + src[...].astype(F32)).astype(BF)
            return

        @pl.loop(0, total)
        def _(i):
            index = (i,) if len(lead) == 1 else (i // lead[1], i % lead[1])
            dst[index] = (dst[index].astype(F32) + src[index].astype(F32)).astype(BF)

    def reduce_scatter(k, p, me, plus, minus, blk, half):
        _, n, shape, half_shape = RS_PHASES[k][p]
        buf = lambda way, slot: s[("rs", k, p, way, slot)]
        reach = n // 2
        top = around(me, reach, n)
        if half is None:
            up, dn = send(blk(top), buf(0, 0), plus), None
        else:
            up, dn = send(half(top, 0), buf(0, 0), plus), send(half(top, 1), buf(1, 0), minus)
        yield
        for slot, d in enumerate(range(reach - 1, 0, -1)):
            a, b = around(me, d, n), around(me, -d, n)
            begin = slot == 0 and half is not None
            up.wait_recv()
            add_block(half(a, 0) if begin else blk(a), buf(0, slot), half_shape if begin else shape)
            up = send(blk(a), buf(0, slot + 1), plus)
            if dn is not None:
                dn.wait_recv()
                add_block(half(b, 1) if begin else blk(b), buf(1, slot), half_shape if begin else shape)
            dn = send(blk(b), buf(1, slot + 1), minus)
            yield
        up.wait_recv()
        add_block(blk(me), buf(0, reach - 1), shape)
        dn.wait_recv()
        add_block(blk(me), buf(1, reach - 1), shape)

    def scatter_colour(k):
        n0 = order_k.index(k) * 2
        for lo in (0, 1):
            handed[n0 + lo].wait_recv()
            for g in (0, 1):
                add_block(OUT.at[k, lo * 2 + g], SIB.at[k, lo * 2 + g], (4, 8, 16, WIDTH))
        if k == 0:
            views = (
                (lambda i: OUT.at[0, xperm(i)], lambda i, g: OUT.at[0, xperm(i), pl.ds(2 * g, 2)]),
                (lambda i: OUT.at[0, xp, i], lambda i, g: OUT.at[0, xp, i, pl.ds(4 * g, 4)]),
                (lambda i: OUT.at[0, xp, y, i], None),
            )
        elif k == 1:
            views = (
                (lambda i: OUT.at[1, :, i], lambda i, g: OUT.at[1, pl.ds(2 * g, 2), i]),
                (lambda i: OUT.at[1, :, y, i], lambda i, g: OUT.at[1, pl.ds(2 * g, 2), y, i]),
                (lambda i: OUT.at[1, xperm(i), y, z], None),
            )
        else:
            views = (
                (lambda i: OUT.at[2, :, :, i], lambda i, g: OUT.at[2, pl.ds(2 * g, 2), :, i]),
                (lambda i: OUT.at[2, xperm(i), :, z], lambda i, g: OUT.at[2, xperm(i), pl.ds(2 * g, 2), z]),
                (lambda i: OUT.at[2, xp, i, z], None),
            )
        for p, (blk, half) in enumerate(views):
            me, _, plus, minus = steps[RS_PHASES[k][p][0]]
            yield from reduce_scatter(k, p, me, plus, minus, blk, half)

    rgens = [scatter_colour(2), scatter_colour(1), scatter_colour(0)]
    pump(rgens, 1)

    for copy in fg:
        copy.wait_recv()
    for j, (cc, k, lo) in enumerate(use):
        ck = half_of[cc] * 3 + k
        cols = pl.ds(pl.multiple_of(order_b[j] * WIDTH, WIDTH), WIDTH)

        @pl.loop(0, 4)
        def _(t, ck=ck, lo=lo, cols=cols, j=j):
            rows = rows_of(t)
            gt = tile(G, ck, lo, t)
            hg = dot(gt, s["DOWN"][:, cols], 1, 1)
            lr = dot(gt, s["L2"][:, cols], 1, 1)
            if j == 0:
                s["H"][rows, :] = hg
                s["A64"][rows, :] = lr
            else:
                s["H"][rows, :] += hg
                s["A64"][rows, :] += lr

        if j % 3 == 2:
            pump(rgens, 1)

    @pl.loop(0, 4)
    def _(t):
        rows = rows_of(t)
        mask = s["MK"][rows, 0:64]
        cl = (s["A64"][rows, :] * s["MK"][rows, 64:128]).astype(BF)
        s["C"][rows, :] = cl
        p = s["PB"][rows, :]
        dh = s["H"][rows, :] * jnp.concatenate([p, p], axis=1) + SCALE * dot(cl, g2t[...])
        gate = s["ACC"][rows, 0:256]
        sg = jax.nn.sigmoid(gate)
        dg = (dh * s["ACC"][rows, 256:512] * sg * (1.0 + gate * (1.0 - sg))).astype(BF)
        s["DG"][rows, :] = dg
        r = dot(dg, l1[...], 1, 1) * mask
        zr = jnp.concatenate([s["ZP"][rows, :], r], axis=1).T
        z16 = zr[0:16] + zr[16:32] + zr[32:48] + zr[48:64]
        r16 = zr[64:80] + zr[80:96] + zr[96:112] + zr[112:128]
        s["ZR"][t] = jnp.concatenate([z16, r16], axis=0)

    def exchange():
        s["AX"][x] = s["ZR"][x]
        got = [send(s["ZR"].at[around(x, d, 4)], s["AX"].at[x], xdev[d]) for d in (1, 2, 3)]
        yield
        for copy in got:
            copy.wait_recv()
        total = s["AX"][0] + s["AX"][1] + s["AX"][2] + s["AX"][3]
        for q in range(4):
            s["YS"][q] = total[q * 8:q * 8 + 8]
        s["AY"][y] = s["YS"][y]
        got = [send(s["YS"].at[around(y, d, 4)], s["AY"].at[y], ydev[d]) for d in (1, 2, 3)]
        yield
        for copy in got:
            copy.wait_recv()
        s["HS"][...] = s["AY"][0] + s["AY"][1] + s["AY"][2] + s["AY"][3]
        got = send(s["HS"], s["HR"], far)
        yield
        got.wait_recv()
        s["FY"][y] = s["HS"][...] + s["HR"][...]
        got = [send(s["FY"].at[y], s["FY"].at[y], ydev[d]) for d in (1, 2, 3)]
        yield
        for copy in got:
            copy.wait_recv()
        s["FX"][x] = s["FY"][...]
        got = [send(s["FY"], s["FX"].at[x], xdev[d]) for d in (1, 2, 3)]
        yield
        for copy in got:
            copy.wait_recv()

    zgens = [exchange()]
    pump(zgens, 1)
    pump(rgens, 1)
    o_gl[...] = (SCALE * dot(s["A"][...], s["DG"][...], 0, 0)).astype(BF)
    pump(zgens, 1)
    o_dd[...] = (SCALE * dot(s["C"][...], s["HID"][...], 0, 0)).astype(BF)
    pump(rgens, 1)
    while zgens:
        pump(zgens, 1)
        pump(rgens, 1)

    for t in range(4):
        cols = slice(t * TILE, t * TILE + TILE)
        mt = s["MK"][t * TILE:t * TILE + TILE, :].T
        z16 = s["FX"][t, 0:2].reshape(16, TILE)
        r16 = s["FX"][t, 2:4].reshape(16, TILE)
        s["LZ"][:, cols] = (jnp.concatenate([z16] * 4, axis=0) * mt[64:128]).astype(BF)
        full = jnp.concatenate([r16] * 4, axis=0) * mt[0:64]
        top = full.astype(BF)
        s["LR"][0:64, cols] = top
        s["LR"][64:128, cols] = (full - top.astype(F32)).astype(BF)

    for n in range(6):
        for lo in (0, 1):
            cols = slice((lo * 6 + n) * WIDTH, (lo * 6 + n + 1) * WIDTH)
            gt = G[n, lo * 2:lo * 2 + 2].reshape(1024, WIDTH)
            o_dl[:, cols] = (SCALE * dot(s["LZ"][...], gt)).astype(BF)
            xt = X[n, lo * 2:lo * 2 + 2].reshape(1024, WIDTH)
            r = dot(s["LR"][...], xt)
            o_gd[:, cols] = (SCALE * (r[0:64] + r[64:128])).astype(BF)
        pump(rgens, 1)
    while rgens:
        pump(rgens, 1)

    for k in range(3):
        done = OUT[k, xp, y, z].astype(F32)
        for q in range(4):
            s["S32"][q, :, k * WIDTH:(k + 1) * WIDTH] = done[q * 4:q * 4 + 4]
    last = [send(s["S32"].at[g], s["MX"].at[grp], d) for g, d in mates]
    s["MX"][grp] = s["S32"][grp]
    for copy in last:
        copy.wait_recv()
    for q in range(4):
        mixed[:, q * 1536:(q + 1) * 1536] = s["MX"][q].astype(BF)
    for copy in pending:
        copy.wait_send()


def local(tokens, out_grad, routes, tasks, route_probs, gate, up, down, g1, l1, g2, l2):
    probs = []
    for j in range(2):
        p = route_probs[:, j]
        hi = lax.reduce_precision(p, 8, 7)
        mid = lax.reduce_precision(p - hi, 8, 7)
        probs += [hi, mid, p - hi - mid]
    fields = [routes[:, 0].astype(F32), routes[:, 1].astype(F32), tasks.astype(F32)] + probs
    meta = jnp.concatenate([f[:, None] for f in fields] + [jnp.zeros((4, 128 - len(fields)), F32)], axis=1)
    shapes = scratch()
    vmem = pl.BlockSpec(memory_space=pltpu.VMEM)
    hbm = pl.BlockSpec(memory_space=pl.ANY)
    mixed, gd, gl, dd, dl = pl.pallas_call(
        functools.partial(body, tuple(shapes)),
        out_shape=(
            jax.ShapeDtypeStruct((4, 6144), BF),
            jax.ShapeDtypeStruct((64, 6144), BF),
            jax.ShapeDtypeStruct((64, 256), BF),
            jax.ShapeDtypeStruct((64, 256), BF),
            jax.ShapeDtypeStruct((64, 6144), BF),
        ),
        in_specs=[vmem, vmem, vmem, hbm, hbm, hbm, hbm, vmem, vmem, hbm],
        out_specs=(vmem,) * 5,
        scratch_shapes=list(shapes.values()),
        compiler_params=pltpu.CompilerParams(
            collective_id=0, has_side_effects=True, vmem_limit_bytes=64 * 2**20 - 2**18
        ),
        cost_estimate=pl.CostEstimate(flops=24 * 10**9, bytes_accessed=12 * 10**6, transcendentals=10**6),
    )(tokens, out_grad, meta, gate[0], up[0], down[0], g1[0].T, l1[0], g2[0].T, l2[0])
    return mixed, gd.T[None], gl[None], dd.T[None], dl[None]


def solution(mesh):
    rows = P(("dp", "expert", "tensor"), None)
    return jax.shard_map(
        local,
        mesh=mesh,
        in_specs=(
            rows,
            rows,
            rows,
            P(("dp", "expert", "tensor")),
            rows,
            P("expert", None, ("dp", "tensor")),
            P("expert", None, ("dp", "tensor")),
            P("expert", ("dp", "tensor"), None),
            P("expert", None, None),
            P("expert", None, ("dp", "tensor")),
            P("expert", ("dp", "tensor"), None),
            P("expert", None, None),
        ),
        out_specs=(
            rows,
            P("expert", None, None),
            P("expert", None, ("dp", "tensor")),
            P("expert", ("dp", "tensor"), None),
            P("expert", None, None),
        ),
        check_vma=False,
    )
```

```python
import functools

import jax
import jax.numpy as jnp
from jax import lax
from jax.experimental import pallas as pl
from jax.experimental.pallas import tpu as pltpu
from jax.sharding import PartitionSpec as P

RANK = 16
SCALE = 0.5
MESH = pl.DeviceIdType.MESH
BF = jnp.bfloat16
F32 = jnp.float32
WIDTH = 512
TILE = 256
MAX_COPIES = 440

ORDER = (("z", "y", "x"), ("z", "x", "y"), ("y", "x", "z"))
SIZE = {"x": 4, "y": 4, "z": 8}
SUB = ((8, 16, WIDTH), (8, 16, WIDTH), (4, 16, WIDTH))
OFFSETS = {4: (0, -1, 1, 2), 8: (0, -1, 1, -2, 2, -3, 3, 4)}


def rs_buffers():
    shapes = {}
    for k in range(3):
        first, second, third = ORDER[k]
        sub = SUB[k]
        reach = SIZE[third] // 2
        for i, r in enumerate(OFFSETS[SIZE[second]]):
            for d in range(1, reach + 1):
                for sign in "+-":
                    if d < reach or sign == "+-"[i % 2]:
                        shapes[("rs", k, 2, r, sign, d)] = pltpu.VMEM(sub, BF)
        for o in OFFSETS[SIZE[second]][1:]:
            shapes[("rs", k, 1, o)] = pltpu.VMEM(sub, BF)
        for o in OFFSETS[SIZE[first]][1:]:
            shapes[("rs", k, 0, o)] = pltpu.VMEM((16, WIDTH), BF)
    return shapes


class Plan:
    RATE = {"x+": 0.046, "x-": 0.046, "y+": 0.046, "y-": 0.046, "z+": 0.046, "z-": 0.046, "c": 0.4}
    DELAY = 2.5

    def __init__(self):
        self.tasks = []

    def add(self, run, deps=(), cost=0.15, rank=5.0, sends=()):
        task = {"run": run, "deps": list(deps), "cost": cost, "rank": rank, "sends": list(sends)}
        self.tasks.append(task)
        return ("task", len(self.tasks) - 1)

    def order(self):
        when, free, now, done = {}, {}, 0.0, []
        left = list(range(len(self.tasks)))
        while left:
            best = None
            for i in left:
                task = self.tasks[i]
                if any(d not in when for d in task["deps"]):
                    continue
                at = max([when[d] for d in task["deps"]] + [0.0])
                key = (max(at, now), task["rank"], i)
                if best is None or key < best[0]:
                    best = (key, i)
            (begin, _, _), i = best
            task = self.tasks[i]
            now = begin + task["cost"]
            when[("task", i)] = now
            for name, link, size in task["sends"]:
                start = max(now, free.get(link, 0.0))
                free[link] = start + size * 1e-6 / self.RATE[link]
                when[name] = free[link] + self.DELAY
            done.append(i)
            left.remove(i)
        self.length = now
        return done


def scratch():
    shapes = {
        "X": pltpu.VMEM((6, 4, 4, 8, 16, WIDTH), BF),
        "G": pltpu.VMEM((6, 4, 4, 8, 16, WIDTH), BF),
        "OUT": pltpu.VMEM((3, 4, 4, 8, 16, WIDTH), BF),
        "DOWN": pltpu.VMEM((256, 6144), BF),
        "WG": pltpu.VMEM((3, 2, 2, 4, 8, 16, 256), BF),
        "WU": pltpu.VMEM((3, 2, 2, 4, 8, 16, 256), BF),
        "G1T": pltpu.VMEM((64, 6144), BF),
        "L2": pltpu.VMEM((64, 6144), BF),
        "ACC": pltpu.VMEM((1024, 512), F32),
        "A64": pltpu.VMEM((1024, 64), F32),
        "C64": pltpu.VMEM((1024, 64), F32),
        "H": pltpu.VMEM((1024, 256), F32),
        "MK": pltpu.VMEM((1024, 128), F32),
        "PB": pltpu.VMEM((1024, 128), F32),
        "ZP": pltpu.VMEM((1024, 64), F32),
        "HID": pltpu.VMEM((1024, 256), BF),
        "DG": pltpu.VMEM((1024, 256), BF),
        "A": pltpu.VMEM((1024, 64), BF),
        "ZS": pltpu.VMEM((1024, 64), BF),
        "C": pltpu.VMEM((1024, 64), BF),
        "T32": pltpu.VMEM((2, 4, 4, 1536), F32),
        "M32": pltpu.VMEM((4, 128), F32),
        "R": pltpu.VMEM((2, 4, 4, 1536), F32),
        "MR": pltpu.VMEM((4, 4, 128), F32),
        "F": pltpu.VMEM((2, 16, 1536), F32),
        "FM": pltpu.VMEM((16, 128), F32),
        "MZ": pltpu.VMEM((8, 16, 128), BF),
        "MF": pltpu.VMEM((2, 4, 16, 128), BF),
        "ZR": pltpu.VMEM((4, 32, 256), F32),
        "AX": pltpu.VMEM((4, 32, 256), F32),
        "YS": pltpu.VMEM((4, 8, 256), F32),
        "AY": pltpu.VMEM((4, 8, 256), F32),
        "HS": pltpu.VMEM((8, 256), F32),
        "HR": pltpu.VMEM((8, 256), F32),
        "FY": pltpu.VMEM((4, 8, 256), F32),
        "FX": pltpu.VMEM((4, 4, 8, 256), F32),
        "LZ": pltpu.VMEM((64, 1024), BF),
        "LR": pltpu.VMEM((128, 1024), BF),
        "S32": pltpu.VMEM((4, 4, 1536), F32),
        "MX": pltpu.VMEM((4, 4, 1536), F32),
        "send": pltpu.SemaphoreType.DMA((MAX_COPIES,)),
        "recv": pltpu.SemaphoreType.DMA((MAX_COPIES,)),
        "local": pltpu.SemaphoreType.DMA((8,)),
    }
    shapes.update(rs_buffers())
    return shapes


def dot(a, b, ca=1, cb=0):
    return lax.dot_general(a, b, (((ca,), (cb,)), ((), ())), preferred_element_type=F32)


def body(names, tok, og, meta, wg, wu, down, g1t, l1, g2t, l2, mixed, o_gd, o_gl, o_dd, o_dl, *refs):
    s = dict(zip(names, refs))
    X, G, OUT = s["X"], s["G"], s["OUT"]
    dp, ex, x = lax.axis_index("dp"), lax.axis_index("expert"), lax.axis_index("tensor")
    h, y = dp // 4, dp % 4
    zl, c = ex // 2, ex % 2
    z = h * 4 + zl
    xlo, xhi = x % 2, x // 2
    xp = xlo * 2 + xhi
    grp = xlo * 2 + c

    def device(x_, y_, z_, c_):
        return ((z_ // 4) * 4 + y_, (z_ % 4) * 2 + c_, x_)

    def around(v, d, n):
        return lax.rem(v + (d + n), n)

    def xperm(i):
        return lax.rem(i, 2) * 2 + i // 2

    xdev = [device(around(x, d, 4), y, z, c) for d in range(4)]
    ydev = [device(x, around(y, d, 4), z, c) for d in range(4)]
    zdev = {1: device(x, y, around(z, 1, 8), c), -1: device(x, y, around(z, -1, 8), c)}
    far = device(x, y, around(z, 4, 8), c)
    sibling = device(x, y, z, 1 - c)
    xpair = xhi * 2 + (1 - xlo)
    pair = device(xpair, y, z, c)
    pair_sibling = device(xpair, y, z, 1 - c)
    ring = {"x": (x, xdev[1], xdev[3]), "y": (y, ydev[1], ydev[3]), "z": (z, zdev[1], zdev[-1])}
    at_offset = {
        "x": {o: xdev[o % 4] for o in OFFSETS[4]},
        "y": {o: ydev[o % 4] for o in OFFSETS[4]},
        "z": {o: device(x, y, around(z, o, 8), c) for o in OFFSETS[8]},
    }
    plan = Plan()
    copies, waited, pending = {}, set(), []

    def send(name, src, dst, target):
        i = len(copies)
        copy = pltpu.make_async_remote_copy(
            src_ref=src, dst_ref=dst, send_sem=s["send"].at[i], recv_sem=s["recv"].at[i],
            device_id=target, device_id_type=MESH,
        )
        copy.start()
        copies[name] = copy
        pending.append(copy)

    local_down = pltpu.make_async_copy(down, s["DOWN"], s["local"].at[0])
    local_g1 = pltpu.make_async_copy(g1t, s["G1T"], s["local"].at[1])
    local_l2 = pltpu.make_async_copy(l2, s["L2"], s["local"].at[2])

    local_wg = pltpu.make_async_copy(wg, s["WG"], s["local"].at[3])
    local_wu = pltpu.make_async_copy(wu, s["WU"], s["local"].at[4])

    barrier = pltpu.get_barrier_semaphore()
    greeted = xdev[1:] + ydev[1:] + [at_offset["z"][o] for o in OFFSETS[8][1:]] + [sibling, pair_sibling]
    for target in greeted:
        pl.semaphore_signal(barrier, inc=1, device_id=target, device_id_type=MESH)
    local_down.start()
    local_g1.start()
    local_l2.start()
    local_wg.start()
    local_wu.start()
    for q in range(4):
        s["T32"][0, q] = tok[:, q * 1536:(q + 1) * 1536].astype(F32)
        s["T32"][1, q] = og[:, q * 1536:(q + 1) * 1536].astype(F32)
    s["M32"][...] = meta[...].astype(F32)
    pl.semaphore_wait(barrier, len(greeted))

    mates = ((xlo * 2 + 1 - c, sibling), ((1 - xlo) * 2 + c, pair), ((1 - xlo) * 2 + 1 - c, pair_sibling))
    for name, src, dst in (("t0", "T32", "R"), ("m", "M32", "MR"), ("t1", "T32", "R")):
        for i, (g, d) in enumerate(mates):
            if name == "m":
                send((name, i), s["M32"], s["MR"].at[grp], d)
            else:
                a = int(name[1])
                send((name, i), s["T32"].at[a, g], s["R"].at[a, grp], d)
    s["R"][0, grp] = s["T32"][0, grp]
    s["R"][1, grp] = s["T32"][1, grp]
    s["MR"][grp] = s["M32"][...]
    s["ACC"][...] = jnp.zeros((1024, 512), F32)
    s["A64"][...] = jnp.zeros((1024, 64), F32)
    s["C64"][...] = jnp.zeros((1024, 64), F32)
    s["H"][...] = jnp.zeros((1024, 256), F32)
    arrived_first = plan.add(lambda: None, cost=0.0, sends=[((n, i), "c", 1000) for n in ("t0", "m", "t1") for i in range(3)])

    def own_block(a, buf):
        def run():
            for q in range(4):
                s["F"][a, q * 4:q * 4 + 4, :] = s["R"][a, q]
            for k in range(3):
                buf[c * 3 + k, xp, y, z] = s["F"][a, :, k * WIDTH:(k + 1) * WIDTH].astype(BF)

        return plan.add(run, deps=[("t%d" % a, i) for i in range(3)], cost=0.5, rank=1)

    def views(buf, lead, k):
        if k == 0:
            return (
                lambda i: buf.at[lead, xp, y, i],
                lambda i: buf.at[lead, xp, i],
                lambda i2, i1: buf.at[lead, xperm(i2), i1],
            )
        if k == 1:
            return (
                lambda i: buf.at[lead, xp, y, i],
                lambda i: buf.at[lead, xperm(i), y],
                lambda i2, i1: buf.at[lead, xperm(i1), i2],
            )
        return (
            lambda i: buf.at[lead, xp, i, z],
            lambda i: buf.at[lead, xperm(i), :, z],
            lambda i2, i1: buf.at[lead, xperm(i1), :, i2],
        )

    def ring_gather(name, axis, blk, size, dep, via, rank):
        me, plus, minus = ring[axis]
        n = SIZE[axis]
        reach = n // 2
        have = {0: list(dep)}
        for d in range(reach):
            for sign, to in (("+", plus), ("-", minus)):
                if d == reach - 1 and via != sign:
                    continue
                mine = around(me, -d if sign == "+" else d, n)
                deps = dep if d == 0 else [name + (sign, d)]
                key = name + (sign, d + 1)

                def run(key=key, mine=mine, to=to):
                    send(key, blk(mine), blk(mine), to)

                plan.add(run, deps=deps, cost=0.1, rank=rank, sends=[(key, axis + sign, size)])
                have[reach if d == reach - 1 else (-(d + 1) if sign == "+" else d + 1)] = [key]
        return have

    def direct_gather(name, axis, blk, size, dep, rank):
        me, n = ring[axis][0], SIZE[axis]
        have = {0: list(dep)}
        for o in OFFSETS[n][1:]:
            key = name + (o,)

            def run(key=key, o=o):
                send(key, blk(me), blk(me), at_offset[axis][o])

            link = axis + ("+" if o > 0 else "-")
            plan.add(run, deps=dep, cost=0.1, rank=rank, sends=[(key, link, size * abs(o))])
            have[o if 2 * o == n else -o] = [key]
        return have

    def gather(a, buf, k, dep, gate1, gate2, rank):
        ck = c * 3 + k
        axis0, axis1, axis2 = ORDER[k]
        blk0, blk1, sub = views(buf, ck, k)
        piece = 16 * WIDTH * 2
        have0 = direct_gather((a, k, 0), axis0, blk0, piece, dep + gate1, rank)
        dep1 = [d for v in have0.values() for d in v]
        size1 = piece * SIZE[axis0]
        have1 = direct_gather((a, k, 1), axis1, blk1, size1, dep1, rank)
        own, other = {}, {}
        me1, me2, n1, n2 = ring[axis1][0], ring[axis2][0], SIZE[axis1], SIZE[axis2]
        for i, r in enumerate(OFFSETS[n1]):
            i1 = around(me1, r, n1)
            have2 = ring_gather(
                (a, k, 2, r), axis2, lambda i2, i1=i1: sub(i2, i1), size1, have1[r] + gate2, "+-"[i % 2],
                rank + 0.01 * i,
            )
            for o, deps in have2.items():
                own[(r, o)] = deps
                if k < 2:
                    key = ("f", a, k, r, o)

                    def run(key=key, i1=i1, o=o):
                        ref = sub(around(me2, o, n2), i1)
                        send(key, ref, ref, sibling)

                    plan.add(run, deps=deps, cost=0.12, rank=rank + 0.5, sends=[(key, "c", size1)])
                    other[(r, o)] = [key]
        if k == 2:
            for o in OFFSETS[n2]:
                key = ("f", a, k, o)

                def run(key=key, o=o):
                    ref = buf.at[ck, :, :, around(me2, o, n2)]
                    send(key, ref, ref, sibling)

                deps = [d for r in OFFSETS[n1] for d in own[(r, o)]]
                plan.add(run, deps=deps, cost=0.12, rank=rank + 0.5, sends=[(key, "c", size1 * 4)])
                for r in OFFSETS[n1]:
                    other[(r, o)] = [key]
        return own, other

    own_x, own_g = own_block(0, X), own_block(1, G)
    got_x = [gather("x", X, k, [own_x], [], [], 1) for k in range(3)]
    gates = []
    for k in range(3):
        near = [got_x[k][0][(r, o)] for r in OFFSETS[SIZE[ORDER[k][1]]] for o in (-1, 1)]
        gates.append([d for v in near for d in v])
    got_g = [
        gather("g", G, k, [own_g], [], gates[k], 2) for k in range(3)
    ]

    def meta_own():
        for q in range(4):
            s["FM"][q * 4:q * 4 + 4, :] = s["MR"][q]
        s["MZ"][z] = pltpu.roll(s["FM"][...], z * 16, 1).astype(BF)

    def meta_sum():
        total = s["MZ"][0].astype(F32)
        for i in range(1, 8):
            total = total + s["MZ"][i].astype(F32)
        s["MF"][xhi, y] = total.astype(BF)

    t = plan.add(meta_own, deps=[("m", i) for i in range(3)], cost=0.3, rank=3)
    have = direct_gather(("mz",), "z", lambda i: s["MZ"].at[i], 4096, [t], 3)
    t = plan.add(meta_sum, deps=[d for v in have.values() for d in v], cost=0.3, rank=3)
    have = direct_gather(("my",), "y", lambda i: s["MF"].at[xhi, i], 4096, [t], 3)
    t = plan.add(
        lambda: send("mx", s["MF"].at[xhi], s["MF"].at[xhi], xdev[2]),
        deps=[d for v in have.values() for d in v], rank=3, sends=[("mx", "x+", 16384)],
    )

    def masks():
        fields = s["MF"][...].astype(F32).reshape(128, 128)
        me_f = ex.astype(F32)
        band = (lax.broadcasted_iota(jnp.int32, (128, 64), 1) // RANK).astype(F32)
        for i in range(8):
            f = fields if i == 0 else pltpu.roll(fields, 128 - 16 * i, 1)
            hit0 = jnp.where(f[:, 0:1] == me_f, 1.0, 0.0)
            hit1 = jnp.where(f[:, 1:2] == me_f, 1.0, 0.0)
            p0 = f[:, 3:4] + f[:, 4:5] + f[:, 5:6]
            p1 = f[:, 6:7] + f[:, 7:8] + f[:, 8:9]
            p = hit0 * p0 + hit1 * p1
            mask = jnp.where(f[:, 2:3] == band, 1.0, 0.0) * (hit0 + hit1)
            both = jnp.concatenate([mask, mask * p], axis=1)
            wide = jnp.broadcast_to(p, (128, 128))
            for g in range(8):
                rows = slice((g * 8 + i) * 16, (g * 8 + i) * 16 + 16)
                s["MK"][rows, :] = both[g * 16:g * 16 + 16, :]
                s["PB"][rows, :] = wide[g * 16:g * 16 + 16, :]

    masked = plan.add(masks, deps=["mx", t], cost=2.0, rank=6)

    loaded = plan.add(lambda: [copy.wait() for copy in (local_wg, local_wu, local_g1)], cost=0.1, rank=7)
    loaded2 = plan.add(lambda: [copy.wait() for copy in (local_down, local_l2)], cost=0.1, rank=7)
    halves = (c, 1 - c)

    def needed(got, which, k, d):
        found = got[k][which]
        if k == 0:
            keys = [found[(r, d)] for r in OFFSETS[4]]
        else:
            keys = [found[(d, o)] for o in OFFSETS[SIZE[ORDER[k][2]]]]
        return [dep for v in keys for dep in v]

    def block(which, k, d):
        at = around(x, d, 4)
        ck = halves[which] * 3 + k
        rows = pl.ds(pl.multiple_of((at // 2) * 512, 512), 512)
        return ck, xperm(at), lax.rem(at, 2) * 6 + ck, rows

    forward, backward = [], []
    for k in range(3):
        for which in (0, 1):
            for d in OFFSETS[4]:

                def fwd(k=k, which=which, d=d):
                    ck, xi, b, rows = block(which, k, d)

                    @pl.loop(0, 2)
                    def _(i):
                        xt = X[ck, xi, :, :, :, pl.ds(pl.multiple_of(i * 256, 256), 256)].reshape(512, 256)
                        at = (b // 4, (b // 2) % 2, b % 2, pl.ds(i * 2, 2))
                        s["ACC"][rows, 0:256] += dot(xt, s["WG"][at].reshape(256, 256))
                        s["ACC"][rows, 256:512] += dot(xt, s["WU"][at].reshape(256, 256))
                        cols = pl.ds(pl.multiple_of(b * WIDTH + i * 256, 256), 256)
                        s["A64"][rows, :] += dot(xt, s["G1T"][:, cols], 1, 1)

                def bwd(k=k, which=which, d=d):
                    ck, xi, b, rows = block(which, k, d)

                    @pl.loop(0, 2)
                    def _(i):
                        gt = G[ck, xi, :, :, :, pl.ds(pl.multiple_of(i * 256, 256), 256)].reshape(512, 256)
                        cols = pl.ds(pl.multiple_of(b * WIDTH + i * 256, 256), 256)
                        s["H"][rows, :] += dot(gt, s["DOWN"][:, cols], 1, 1)
                        s["C64"][rows, :] += dot(gt, s["L2"][:, cols], 1, 1)

                forward.append(plan.add(fwd, deps=needed(got_x, which, k, d) + [loaded], cost=0.9, rank=10))
                backward.append(plan.add(bwd, deps=needed(got_g, which, k, d) + [loaded2], cost=0.8, rank=20))

    active = []
    for t in range(4):

        def act(t=t):
            rows = slice(t * TILE, t * TILE + TILE)
            mask = s["MK"][rows, 0:64]
            a = (s["A64"][rows, :] * mask).astype(BF)
            gate = s["ACC"][rows, 0:256] + SCALE * dot(a, l1[...])
            s["ACC"][rows, 0:256] = gate
            s["A"][rows, :] = a
            hid = (gate * jax.nn.sigmoid(gate) * s["ACC"][rows, 256:512]).astype(BF)
            s["HID"][rows, :] = hid
            zp = dot(hid, g2t[...], 1, 1) * mask
            s["ZP"][rows, :] = zp
            s["ZS"][rows, :] = (SCALE * zp).astype(BF)

        active.append(plan.add(act, deps=forward + [masked], cost=1.0, rank=11))

    def out_rows(cols, t):
        rows = pl.ds(pl.multiple_of(t * TILE, TILE), TILE)
        o = dot(s["HID"][rows, :], s["DOWN"][:, cols]) + dot(s["ZS"][rows, :], s["L2"][:, cols])
        p = s["PB"][rows, :]
        return o * jnp.concatenate([p, p, p, p], axis=1)

    order_k = (2, 0, 1)
    out_of = {}
    for n, (k, lo) in enumerate([(k, lo) for k in order_k for lo in (0, 1)]):

        def theirs(n=n, k=k, lo=lo):
            b = lo * 6 + halves[1] * 3 + k
            cols = pl.ds(pl.multiple_of(b * WIDTH, WIDTH), WIDTH)

            stage = s["WG" if n < 3 else "WU"].at[n % 3]

            @pl.loop(0, 4)
            def _(t):
                o = out_rows(cols, t).astype(BF)
                for f in (0, 1):
                    half = o[:, f * 256:f * 256 + 256].reshape(2, 8, 16, 256)
                    stage[f, t // 2, pl.ds((t % 2) * 2, 2)] = half

            for f in (0, 1):
                dst = OUT.at[k, pl.ds(lo * 2, 2), :, :, :, pl.ds(f * 256, 256)]
                send(("o", k, lo, f), stage.at[f], dst, sibling)

        plan.add(
            theirs, deps=active + [loaded2], cost=1.6, rank=12 + 0.1 * n,
            sends=[(("o", k, lo, f), "c", 2**19) for f in (0, 1)],
        )

    for n, (k, lo) in enumerate([(k, lo) for k in order_k for lo in (0, 1)]):

        def ours(n=n, k=k, lo=lo):
            b = lo * 6 + halves[0] * 3 + k
            cols = pl.ds(pl.multiple_of(b * WIDTH, WIDTH), WIDTH)

            @pl.loop(0, 4)
            def _(t):
                at = (k, lo * 2 + t // 2, pl.ds((t % 2) * 2, 2))
                o = out_rows(cols, t) + OUT[at].reshape(TILE, WIDTH).astype(F32)
                OUT[at] = o.astype(BF).reshape(2, 8, 16, WIDTH)

        out_of[(k, lo)] = plan.add(ours, deps=active + [("o", k, lo, f) for f in (0, 1)], cost=1.6, rank=13 + 0.1 * n)

    def add_block(dst, sources, shape):
        part = shape[0] if len(shape) == 2 else min(4, shape[0])
        for i in range(0, shape[0], part):
            at = pl.ds(i, part)
            total = dst[at].astype(F32)
            for src in sources:
                total = total + src[at].astype(F32)
            dst[at] = total.astype(BF)

    def ring_reduce(name, axis, blk, shape, dep, via, rank):
        me, plus, minus = ring[axis]
        n = SIZE[axis]
        reach = n // 2
        size = 2
        for v in shape:
            size *= v
        chain = {}
        for d in range(reach, 0, -1):
            for sign, to in (("+", plus), ("-", minus)):
                if d == reach and sign != via:
                    continue
                at = around(me, d if sign == "+" else -d, n)
                key = name + (sign, d)
                before = chain.get(sign)

                def run(key=key, at=at, to=to, before=before):
                    if before is not None:
                        add_block(blk(at), [s[before]], shape)
                    send(key, blk(at), s[key], to)

                deps = list(dep) + ([before] if before is not None else [])
                cost = 0.1 if before is None else 0.35
                plan.add(run, deps=deps, rank=rank, cost=cost, sends=[(key, axis + sign, size)])
                chain[sign] = key

        def finish():
            add_block(blk(me), [s[chain[sign]] for sign in "+-"], shape)

        return plan.add(finish, deps=list(dep) + [chain["+"], chain["-"]], cost=0.4, rank=rank)

    def direct_reduce(name, axis, blk, shape, dep, rank):
        me, n = ring[axis][0], SIZE[axis]
        size = 2
        for v in shape:
            size *= v
        keys = []
        for o in sorted(OFFSETS[n][1:], key=lambda o: -abs(o)):
            key = name + (o,)

            def run(key=key, o=o):
                send(key, blk(around(me, o, n)), s[key], at_offset[axis][o])

            link = axis + ("+" if o > 0 else "-")
            plan.add(run, deps=dep(o), rank=rank, cost=0.1, sends=[(key, link, size * abs(o))])
            keys.append(key)

        def finish():
            add_block(blk(me), [s[key] for key in keys], shape)

        return plan.add(finish, deps=dep(0) + keys, cost=0.4, rank=rank)

    def scatter(k):
        axis0, axis1, axis2 = ORDER[k]
        blk0, blk1, sub = views(OUT, k, k)
        ready = [out_of[(k, 0)], out_of[(k, 1)]]
        me1, n1 = ring[axis1][0], SIZE[axis1]
        parts = {}
        for i, r in enumerate(OFFSETS[n1]):
            i1 = around(me1, r, n1)
            parts[r] = ring_reduce(
                ("rs", k, 2, r), axis2, lambda i2, i1=i1: sub(i2, i1), SUB[k], ready, "+-"[i % 2],
                4 - 0.1 * i,
            )
        one = direct_reduce(("rs", k, 1), axis1, blk1, SUB[k], lambda o: [parts[o]], 3)
        return direct_reduce(("rs", k, 0), axis0, blk0, (16, WIDTH), lambda o: [one], 2)

    summed = [scatter(k) for k in order_k]

    reverse = []
    for t in range(4):

        def deact(t=t):
            rows = slice(t * TILE, t * TILE + TILE)
            mask = s["MK"][rows, 0:64]
            cl = (s["C64"][rows, :] * s["MK"][rows, 64:128]).astype(BF)
            s["C"][rows, :] = cl
            p = s["PB"][rows, :]
            dh = s["H"][rows, :] * jnp.concatenate([p, p], axis=1) + SCALE * dot(cl, g2t[...])
            gate = s["ACC"][rows, 0:256]
            sg = jax.nn.sigmoid(gate)
            dg = (dh * s["ACC"][rows, 256:512] * sg * (1.0 + gate * (1.0 - sg))).astype(BF)
            s["DG"][rows, :] = dg
            r = dot(dg, l1[...], 1, 1) * mask
            zr = jnp.concatenate([s["ZP"][rows, :], r], axis=1).T
            z16 = zr[0:16] + zr[16:32] + zr[32:48] + zr[48:64]
            r16 = zr[64:80] + zr[80:96] + zr[96:112] + zr[112:128]
            s["ZR"][t] = jnp.concatenate([z16, r16], axis=0)

        reverse.append(plan.add(deact, deps=backward + active, cost=1.3, rank=21))

    def ex1():
        s["AX"][x] = s["ZR"][x]
        for d in (1, 2, 3):
            send(("e1", d), s["ZR"].at[around(x, d, 4)], s["AX"].at[x], xdev[d])

    def ex2():
        total = s["AX"][0] + s["AX"][1] + s["AX"][2] + s["AX"][3]
        for q in range(4):
            s["YS"][q] = total[q * 8:q * 8 + 8]
        s["AY"][y] = s["YS"][y]
        for d in (1, 2, 3):
            send(("e2", d), s["YS"].at[around(y, d, 4)], s["AY"].at[y], ydev[d])

    def ex3():
        s["HS"][...] = s["AY"][0] + s["AY"][1] + s["AY"][2] + s["AY"][3]
        send(("e3", 1), s["HS"], s["HR"], far)

    def ex4():
        s["FY"][y] = s["HS"][...] + s["HR"][...]
        for d in (1, 2, 3):
            send(("e4", d), s["FY"].at[y], s["FY"].at[y], ydev[d])

    def ex5():
        s["FX"][x] = s["FY"][...]
        for d in (1, 2, 3):
            send(("e5", d), s["FY"], s["FX"].at[x], xdev[d])

    deps = reverse
    for n, (run, axis, size) in enumerate(((ex1, "x", 32768), (ex2, "y", 8192), (ex3, "z", 32768), (ex4, "y", 8192), (ex5, "x", 32768))):
        names = [("e%d" % (n + 1), d) for d in ((1,) if n == 2 else (1, 2, 3))]
        plan.add(run, deps=deps, cost=0.4, rank=0.5, sends=[(m, axis + "+-"[i % 2], size) for i, m in enumerate(names)])
        deps = names

    def lowrank():
        o_gl[...] = (SCALE * dot(s["A"][...], s["DG"][...], 0, 0)).astype(BF)
        o_dd[...] = (SCALE * dot(s["C"][...], s["HID"][...], 0, 0)).astype(BF)

    plan.add(lowrank, deps=reverse, cost=2.0, rank=23)

    def left_sides():
        for t in range(4):
            cols = slice(t * TILE, t * TILE + TILE)
            mt = s["MK"][t * TILE:t * TILE + TILE, :].T
            z16 = s["FX"][t, 0:2].reshape(16, TILE)
            r16 = s["FX"][t, 2:4].reshape(16, TILE)
            s["LZ"][:, cols] = (jnp.concatenate([z16] * 4, axis=0) * mt[64:128]).astype(BF)
            full = jnp.concatenate([r16] * 4, axis=0) * mt[0:64]
            top = full.astype(BF)
            s["LR"][0:64, cols] = top
            s["LR"][64:128, cols] = (full - top.astype(F32)).astype(BF)

    left = plan.add(left_sides, deps=deps, cost=1.5, rank=22)
    for n in range(4):

        def grads(n=n):
            @pl.loop(3 * n, 3 * n + 3)
            def _(b):
                cols = pl.ds(pl.multiple_of(b * WIDTH, WIDTH), WIDTH)
                at = (b % 6, pl.ds((b // 6) * 2, 2))
                o_dl[:, cols] = (SCALE * dot(s["LZ"][...], G[at].reshape(1024, WIDTH))).astype(BF)
                r = dot(s["LR"][...], X[at].reshape(1024, WIDTH))
                o_gd[:, cols] = (SCALE * (r[0:64] + r[64:128])).astype(BF)

        plan.add(grads, deps=[left], cost=2.7, rank=24)

    def give_back():
        for k in range(3):
            done = OUT[k, xp, y, z].astype(F32)
            for q in range(4):
                s["S32"][q, :, k * WIDTH:(k + 1) * WIDTH] = done[q * 4:q * 4 + 4]
        for i, (g, d) in enumerate(mates):
            send(("l", i), s["S32"].at[g], s["MX"].at[grp], d)
        s["MX"][grp] = s["S32"][grp]

    plan.add(give_back, deps=summed, cost=0.5, rank=0, sends=[(("l", i), "c", 24576) for i in range(3)])

    def finish():
        for q in range(4):
            mixed[:, q * 1536:(q + 1) * 1536] = s["MX"][q].astype(BF)

    plan.add(finish, deps=[("l", i) for i in range(3)], cost=0.3, rank=0)

    for i in plan.order():
        task = plan.tasks[i]
        for d in task["deps"]:
            if d in copies and d not in waited:
                copies[d].wait_recv()
                waited.add(d)
        task["run"]()
    for d in copies:
        if d not in waited:
            copies[d].wait_recv()
    for copy in pending:
        copy.wait_send()


def hand_over(*refs):
    for src, dst in zip(refs[:5], refs[5:]):
        dst[...] = src[...]


def local(tokens, out_grad, routes, tasks, route_probs, gate, up, down, g1, l1, g2, l2):
    probs = []
    for j in range(2):
        p = route_probs[:, j]
        hi = lax.reduce_precision(p, 8, 7)
        mid = lax.reduce_precision(p - hi, 8, 7)
        probs += [hi, mid, p - hi - mid]
    fields = [routes[:, 0].astype(F32), routes[:, 1].astype(F32), tasks.astype(F32)] + probs
    meta = jnp.concatenate([f[:, None] for f in fields] + [jnp.zeros((4, 128 - len(fields)), F32)], axis=1)
    shapes = scratch()
    shapes_out = tuple(
        jax.ShapeDtypeStruct(v, BF) for v in ((4, 6144), (64, 6144), (64, 256), (64, 256), (64, 6144))
    )
    w_shape = (3, 2, 2, 4, 8, 16, 256)
    vmem = pl.BlockSpec(memory_space=pltpu.VMEM)
    hbm = pl.BlockSpec(memory_space=pl.ANY)
    mixed, gd, gl, dd, dl = pl.pallas_call(
        functools.partial(body, tuple(shapes)),
        out_shape=shapes_out,
        in_specs=[vmem, vmem, vmem, hbm, hbm, hbm, hbm, vmem, vmem, hbm],
        out_specs=(vmem,) * 5,
        scratch_shapes=list(shapes.values()),
        compiler_params=pltpu.CompilerParams(
            collective_id=0, has_side_effects=True, vmem_limit_bytes=64 * 2**20 - 2**18
        ),
        cost_estimate=pl.CostEstimate(flops=24 * 10**9, bytes_accessed=12 * 10**6, transcendentals=10**6),
    )(tokens, out_grad, meta, gate.reshape(w_shape), up.reshape(w_shape), down[0], g1[0].T, l1[0], g2[0].T, l2[0])
    mixed, gd, gl, dd, dl = pl.pallas_call(
        hand_over, out_shape=shapes_out, in_specs=[vmem] * 5, out_specs=(vmem,) * 5,
    )(mixed, gd, gl, dd, dl)
    return mixed, gd.T[None], gl[None], dd.T[None], dl[None]


def solution(mesh):
    rows = P(("dp", "expert", "tensor"), None)
    return jax.shard_map(
        local,
        mesh=mesh,
        in_specs=(
            rows,
            rows,
            rows,
            P(("dp", "expert", "tensor")),
            rows,
            P("expert", None, ("dp", "tensor")),
            P("expert", None, ("dp", "tensor")),
            P("expert", ("dp", "tensor"), None),
            P("expert", None, None),
            P("expert", None, ("dp", "tensor")),
            P("expert", ("dp", "tensor"), None),
            P("expert", None, None),
        ),
        out_specs=(
            rows,
            P("expert", None, None),
            P("expert", None, ("dp", "tensor")),
            P("expert", ("dp", "tensor"), None),
            P("expert", None, None),
        ),
        check_vma=False,
    )
```

```python
import functools

import jax
import jax.numpy as jnp
from jax import lax
from jax.experimental import pallas as pl
from jax.experimental.pallas import tpu as pltpu
from jax.sharding import PartitionSpec as P

RANK = 16
SCALE = 0.5
MESH = pl.DeviceIdType.MESH
BF = jnp.bfloat16
F32 = jnp.float32
WIDTH = 512
TILE = 256
MAX_COPIES = 440

ORDER = (("z", "y", "x"), ("z", "x", "y"), ("y", "x", "z"))
SIZE = {"x": 4, "y": 4, "z": 8}
SUB = ((8, 16, WIDTH), (8, 16, WIDTH), (4, 16, WIDTH))
OFFSETS = {4: (0, -1, 1, 2), 8: (0, -1, 1, -2, 2, -3, 3, 4)}


def rs_buffers():
    shapes = {}
    for k in range(3):
        first, second, third = ORDER[k]
        sub = SUB[k]
        reach = SIZE[third] // 2
        for i, r in enumerate(OFFSETS[SIZE[second]]):
            for d in range(1, reach + 1):
                for sign in "+-":
                    if d < reach or sign == "+-"[i % 2]:
                        shapes[("rs", k, 2, r, sign, d)] = pltpu.VMEM(sub, BF)
        for o in OFFSETS[SIZE[second]][1:]:
            shapes[("rs", k, 1, o)] = pltpu.VMEM(sub, BF)
        for o in OFFSETS[SIZE[first]][1:]:
            shapes[("rs", k, 0, o)] = pltpu.VMEM((16, WIDTH), BF)
    return shapes


class Plan:
    RATE = {"x+": 0.046, "x-": 0.046, "y+": 0.046, "y-": 0.046, "z+": 0.04, "z-": 0.04, "c": 0.4}
    DELAY = 2.8

    def __init__(self):
        self.tasks = []

    def add(self, run, deps=(), cost=0.15, rank=5.0, sends=()):
        task = {"run": run, "deps": list(deps), "cost": cost, "rank": rank, "sends": list(sends)}
        self.tasks.append(task)
        return ("task", len(self.tasks) - 1)

    def order(self):
        when, free, now, done = {}, {}, 0.0, []
        left = list(range(len(self.tasks)))
        while left:
            best = None
            for i in left:
                task = self.tasks[i]
                if any(d not in when for d in task["deps"]):
                    continue
                at = max([when[d] for d in task["deps"]] + [0.0])
                key = (max(at, now), task["rank"], i)
                if best is None or key < best[0]:
                    best = (key, i)
            (begin, _, _), i = best
            task = self.tasks[i]
            now = begin + task["cost"]
            when[("task", i)] = now
            for name, link, size in task["sends"]:
                start = max(now, free.get(link, 0.0))
                free[link] = start + size * 1e-6 / self.RATE[link]
                when[name] = free[link] + self.DELAY
            done.append(i)
            left.remove(i)
        self.length = now
        return done


def scratch():
    shapes = {
        "X": pltpu.VMEM((6, 4, 4, 8, 16, WIDTH), BF),
        "G": pltpu.VMEM((6, 4, 4, 8, 16, WIDTH), BF),
        "OUT": pltpu.VMEM((3, 4, 4, 8, 16, WIDTH), BF),
        "DOWN": pltpu.VMEM((256, 6144), BF),
        "WG": pltpu.VMEM((3, 2, 2, 4, 8, 16, 256), BF),
        "WU": pltpu.VMEM((3, 2, 2, 4, 8, 16, 256), BF),
        "G1T": pltpu.VMEM((64, 6144), BF),
        "L2": pltpu.VMEM((64, 6144), BF),
        "ACC": pltpu.VMEM((1024, 512), F32),
        "A64": pltpu.VMEM((1024, 64), F32),
        "C64": pltpu.VMEM((1024, 64), F32),
        "H": pltpu.VMEM((1024, 256), F32),
        "MK": pltpu.VMEM((1024, 128), F32),
        "PB": pltpu.VMEM((1024, 128), F32),
        "ZP": pltpu.VMEM((1024, 64), F32),
        "HID": pltpu.VMEM((1024, 256), BF),
        "DG": pltpu.VMEM((1024, 256), BF),
        "A": pltpu.VMEM((1024, 64), BF),
        "ZS": pltpu.VMEM((1024, 64), BF),
        "C": pltpu.VMEM((1024, 64), BF),
        "T32": pltpu.VMEM((2, 4, 4, 1536), F32),
        "M32": pltpu.VMEM((4, 128), F32),
        "R": pltpu.VMEM((2, 4, 4, 1536), F32),
        "MR": pltpu.VMEM((4, 4, 128), F32),
        "F": pltpu.VMEM((2, 16, 1536), F32),
        "FM": pltpu.VMEM((16, 128), F32),
        "MZ": pltpu.VMEM((8, 16, 128), BF),
        "MF": pltpu.VMEM((2, 4, 16, 128), BF),
        "ZR": pltpu.VMEM((4, 32, 256), F32),
        "AX": pltpu.VMEM((4, 32, 256), F32),
        "YS": pltpu.VMEM((4, 8, 256), F32),
        "AY": pltpu.VMEM((4, 8, 256), F32),
        "HS": pltpu.VMEM((8, 256), F32),
        "HR": pltpu.VMEM((8, 256), F32),
        "FY": pltpu.VMEM((4, 8, 256), F32),
        "FX": pltpu.VMEM((4, 4, 8, 256), F32),
        "LZ": pltpu.VMEM((64, 1024), BF),
        "LR": pltpu.VMEM((128, 1024), BF),
        "S32": pltpu.VMEM((4, 4, 1536), F32),
        "MX": pltpu.VMEM((4, 4, 1536), F32),
        "send": pltpu.SemaphoreType.DMA((MAX_COPIES,)),
        "recv": pltpu.SemaphoreType.DMA((MAX_COPIES,)),
        "local": pltpu.SemaphoreType.DMA((8,)),
    }
    shapes.update(rs_buffers())
    return shapes


def dot(a, b, ca=1, cb=0):
    return lax.dot_general(a, b, (((ca,), (cb,)), ((), ())), preferred_element_type=F32)


def body(names, tok, og, meta, wg, wu, down, g1t, l1, g2t, l2, mixed, o_gd, o_gl, o_dd, o_dl, *refs):
    s = dict(zip(names, refs))
    X, G, OUT = s["X"], s["G"], s["OUT"]
    dp, ex, x = lax.axis_index("dp"), lax.axis_index("expert"), lax.axis_index("tensor")
    h, y = dp // 4, dp % 4
    zl, c = ex // 2, ex % 2
    z = h * 4 + zl
    xlo, xhi = x % 2, x // 2
    xp = xlo * 2 + xhi
    grp = xlo * 2 + c

    def device(x_, y_, z_, c_):
        return ((z_ // 4) * 4 + y_, (z_ % 4) * 2 + c_, x_)

    def around(v, d, n):
        return lax.rem(v + (d + n), n)

    def xperm(i):
        return lax.rem(i, 2) * 2 + i // 2

    xdev = [device(around(x, d, 4), y, z, c) for d in range(4)]
    ydev = [device(x, around(y, d, 4), z, c) for d in range(4)]
    zdev = {1: device(x, y, around(z, 1, 8), c), -1: device(x, y, around(z, -1, 8), c)}
    far = device(x, y, around(z, 4, 8), c)
    sibling = device(x, y, z, 1 - c)
    xpair = xhi * 2 + (1 - xlo)
    pair = device(xpair, y, z, c)
    pair_sibling = device(xpair, y, z, 1 - c)
    ring = {"x": (x, xdev[1], xdev[3]), "y": (y, ydev[1], ydev[3]), "z": (z, zdev[1], zdev[-1])}
    at_offset = {
        "x": {o: xdev[o % 4] for o in OFFSETS[4]},
        "y": {o: ydev[o % 4] for o in OFFSETS[4]},
        "z": {o: device(x, y, around(z, o, 8), c) for o in OFFSETS[8]},
    }
    plan = Plan()
    copies, waited, pending = {}, set(), []

    def send(name, src, dst, target):
        i = len(copies)
        copy = pltpu.make_async_remote_copy(
            src_ref=src, dst_ref=dst, send_sem=s["send"].at[i], recv_sem=s["recv"].at[i],
            device_id=target, device_id_type=MESH,
        )
        copy.start()
        copies[name] = copy
        pending.append(copy)

    local_down = pltpu.make_async_copy(down, s["DOWN"], s["local"].at[0])
    local_g1 = pltpu.make_async_copy(g1t, s["G1T"], s["local"].at[1])
    local_l2 = pltpu.make_async_copy(l2, s["L2"], s["local"].at[2])

    local_wg = pltpu.make_async_copy(wg, s["WG"], s["local"].at[3])
    local_wu = pltpu.make_async_copy(wu, s["WU"], s["local"].at[4])

    barrier = pltpu.get_barrier_semaphore()
    greeted = xdev[1:] + ydev[1:] + [at_offset["z"][o] for o in OFFSETS[8][1:]] + [sibling, pair_sibling]
    for target in greeted:
        pl.semaphore_signal(barrier, inc=1, device_id=target, device_id_type=MESH)
    local_down.start()
    local_g1.start()
    local_l2.start()
    local_wg.start()
    local_wu.start()
    for q in range(4):
        s["T32"][0, q] = tok[:, q * 1536:(q + 1) * 1536].astype(F32)
        s["T32"][1, q] = og[:, q * 1536:(q + 1) * 1536].astype(F32)
    s["M32"][...] = meta[...].astype(F32)
    pl.semaphore_wait(barrier, len(greeted))

    mates = ((xlo * 2 + 1 - c, sibling), ((1 - xlo) * 2 + c, pair), ((1 - xlo) * 2 + 1 - c, pair_sibling))
    for name, src, dst in (("t0", "T32", "R"), ("m", "M32", "MR"), ("t1", "T32", "R")):
        for i, (g, d) in enumerate(mates):
            if name == "m":
                send((name, i), s["M32"], s["MR"].at[grp], d)
            else:
                a = int(name[1])
                send((name, i), s["T32"].at[a, g], s["R"].at[a, grp], d)
    s["R"][0, grp] = s["T32"][0, grp]
    s["R"][1, grp] = s["T32"][1, grp]
    s["MR"][grp] = s["M32"][...]
    s["ACC"][...] = jnp.zeros((1024, 512), F32)
    s["A64"][...] = jnp.zeros((1024, 64), F32)
    s["C64"][...] = jnp.zeros((1024, 64), F32)
    s["H"][...] = jnp.zeros((1024, 256), F32)
    arrived_first = plan.add(lambda: None, cost=0.0, sends=[((n, i), "c", 1000) for n in ("t0", "m", "t1") for i in range(3)])

    def own_block(a, buf):
        def run():
            for q in range(4):
                s["F"][a, q * 4:q * 4 + 4, :] = s["R"][a, q]
            for k in range(3):
                buf[c * 3 + k, xp, y, z] = s["F"][a, :, k * WIDTH:(k + 1) * WIDTH].astype(BF)

        return plan.add(run, deps=[("t%d" % a, i) for i in range(3)], cost=0.5, rank=1)

    def views(buf, lead, k):
        if k == 0:
            return (
                lambda i: buf.at[lead, xp, y, i],
                lambda i: buf.at[lead, xp, i],
                lambda i2, i1: buf.at[lead, xperm(i2), i1],
            )
        if k == 1:
            return (
                lambda i: buf.at[lead, xp, y, i],
                lambda i: buf.at[lead, xperm(i), y],
                lambda i2, i1: buf.at[lead, xperm(i1), i2],
            )
        return (
            lambda i: buf.at[lead, xp, i, z],
            lambda i: buf.at[lead, xperm(i), :, z],
            lambda i2, i1: buf.at[lead, xperm(i1), :, i2],
        )

    def ring_gather(name, axis, blk, size, dep, via, rank):
        me, plus, minus = ring[axis]
        n = SIZE[axis]
        reach = n // 2
        have = {0: list(dep)}
        for d in range(reach):
            for sign, to in (("+", plus), ("-", minus)):
                if d == reach - 1 and via != sign:
                    continue
                mine = around(me, -d if sign == "+" else d, n)
                deps = dep if d == 0 else [name + (sign, d)]
                key = name + (sign, d + 1)

                def run(key=key, mine=mine, to=to):
                    send(key, blk(mine), blk(mine), to)

                plan.add(run, deps=deps, cost=0.15, rank=rank, sends=[(key, axis + sign, size)])
                have[reach if d == reach - 1 else (-(d + 1) if sign == "+" else d + 1)] = [key]
        return have

    def direct_gather(name, axis, blk, size, dep, rank):
        me, n = ring[axis][0], SIZE[axis]
        have = {0: list(dep)}
        for o in OFFSETS[n][1:]:
            key = name + (o,)

            def run(key=key, o=o):
                send(key, blk(me), blk(me), at_offset[axis][o])

            link = axis + ("+" if o > 0 else "-")
            plan.add(run, deps=dep, cost=0.15, rank=rank, sends=[(key, link, size * abs(o))])
            have[o if 2 * o == n else -o] = [key]
        return have

    def gather(a, buf, k, dep, gate1, gate2, rank):
        ck = c * 3 + k
        axis0, axis1, axis2 = ORDER[k]
        blk0, blk1, sub = views(buf, ck, k)
        piece = 16 * WIDTH * 2
        have0 = direct_gather((a, k, 0), axis0, blk0, piece, dep + gate1, rank)
        dep1 = [d for v in have0.values() for d in v]
        size1 = piece * SIZE[axis0]
        have1 = direct_gather((a, k, 1), axis1, blk1, size1, dep1, rank)
        own, other = {}, {}
        me1, me2, n1, n2 = ring[axis1][0], ring[axis2][0], SIZE[axis1], SIZE[axis2]
        for i, r in enumerate(OFFSETS[n1]):
            i1 = around(me1, r, n1)
            have2 = ring_gather(
                (a, k, 2, r), axis2, lambda i2, i1=i1: sub(i2, i1), size1, have1[r] + gate2, "+-"[i % 2],
                rank + 0.01 * i,
            )
            for o, deps in have2.items():
                own[(r, o)] = deps
        for o in OFFSETS[n2]:
            key = ("f", a, k, o)

            def run(key=key, o=o):
                i2 = around(me2, o, n2)
                ref = buf.at[ck, xperm(i2)] if k == 0 else buf.at[ck, :, i2] if k == 1 else buf.at[ck, :, :, i2]
                send(key, ref, ref, sibling)

            deps = [d for r in OFFSETS[n1] for d in own[(r, o)]]
            plan.add(run, deps=deps, cost=0.15, rank=rank + 0.5, sends=[(key, "c", size1 * 4)])
            for r in OFFSETS[n1]:
                other[(r, o)] = [key]
        return own, other

    own_x, own_g = own_block(0, X), own_block(1, G)
    got_x = [gather("x", X, k, [own_x], [], [], 1) for k in range(3)]
    gates = []
    for k in range(3):
        near = [got_x[k][0][(r, o)] for r in OFFSETS[SIZE[ORDER[k][1]]] for o in (-1, 1)]
        gates.append([d for v in near for d in v])
    got_g = [
        gather("g", G, k, [own_g], [], gates[k], 2) for k in range(3)
    ]

    def meta_own():
        for q in range(4):
            s["FM"][q * 4:q * 4 + 4, :] = s["MR"][q]
        s["MZ"][z] = pltpu.roll(s["FM"][...], z * 16, 1).astype(BF)

    def meta_sum():
        total = s["MZ"][0].astype(F32)
        for i in range(1, 8):
            total = total + s["MZ"][i].astype(F32)
        s["MF"][xhi, y] = total.astype(BF)

    t = plan.add(meta_own, deps=[("m", i) for i in range(3)], cost=0.3, rank=3)
    have = direct_gather(("mz",), "z", lambda i: s["MZ"].at[i], 4096, [t], 3)
    t = plan.add(meta_sum, deps=[d for v in have.values() for d in v], cost=0.3, rank=3)
    have = direct_gather(("my",), "y", lambda i: s["MF"].at[xhi, i], 4096, [t], 3)
    t = plan.add(
        lambda: send("mx", s["MF"].at[xhi], s["MF"].at[xhi], xdev[2]),
        deps=[d for v in have.values() for d in v], rank=3, sends=[("mx", "x+", 16384)],
    )

    def masks():
        fields = s["MF"][...].astype(F32).reshape(128, 128)
        me_f = ex.astype(F32)
        band = (lax.broadcasted_iota(jnp.int32, (128, 64), 1) // RANK).astype(F32)
        for i in range(8):
            f = fields if i == 0 else pltpu.roll(fields, 128 - 16 * i, 1)
            hit0 = jnp.where(f[:, 0:1] == me_f, 1.0, 0.0)
            hit1 = jnp.where(f[:, 1:2] == me_f, 1.0, 0.0)
            p0 = f[:, 3:4] + f[:, 4:5] + f[:, 5:6]
            p1 = f[:, 6:7] + f[:, 7:8] + f[:, 8:9]
            p = hit0 * p0 + hit1 * p1
            mask = jnp.where(f[:, 2:3] == band, 1.0, 0.0) * (hit0 + hit1)
            both = jnp.concatenate([mask, mask * p], axis=1)
            wide = jnp.broadcast_to(p, (128, 128))
            for g in range(8):
                rows = slice((g * 8 + i) * 16, (g * 8 + i) * 16 + 16)
                s["MK"][rows, :] = both[g * 16:g * 16 + 16, :]
                s["PB"][rows, :] = wide[g * 16:g * 16 + 16, :]

    masked = plan.add(masks, deps=["mx", t], cost=2.0, rank=6)

    loaded = plan.add(lambda: [copy.wait() for copy in (local_wg, local_wu, local_g1)], cost=0.1, rank=7)
    loaded2 = plan.add(lambda: [copy.wait() for copy in (local_down, local_l2)], cost=0.1, rank=7)
    halves = (c, 1 - c)

    def needed(got, which, k, d):
        found = got[k][which]
        if k == 0:
            keys = [found[(r, d)] for r in OFFSETS[4]]
        else:
            keys = [found[(d, o)] for o in OFFSETS[SIZE[ORDER[k][2]]]]
        return [dep for v in keys for dep in v]

    def block(which, k, d):
        at = around(x, d, 4)
        ck = halves[which] * 3 + k
        rows = pl.ds(pl.multiple_of((at // 2) * 512, 512), 512)
        return ck, xperm(at), lax.rem(at, 2) * 6 + ck, rows

    forward, backward = [], []
    for k in range(3):
        for which in (0, 1):
            for d in OFFSETS[4]:

                def fwd(k=k, which=which, d=d):
                    ck, xi, b, rows = block(which, k, d)

                    @pl.loop(0, 2)
                    def _(i):
                        xt = X[ck, xi, :, :, :, pl.ds(pl.multiple_of(i * 256, 256), 256)].reshape(512, 256)
                        at = (b // 4, (b // 2) % 2, b % 2, pl.ds(i * 2, 2))
                        s["ACC"][rows, 0:256] += dot(xt, s["WG"][at].reshape(256, 256))
                        s["ACC"][rows, 256:512] += dot(xt, s["WU"][at].reshape(256, 256))
                        cols = pl.ds(pl.multiple_of(b * WIDTH + i * 256, 256), 256)
                        s["A64"][rows, :] += dot(xt, s["G1T"][:, cols], 1, 1)

                def bwd(k=k, which=which, d=d):
                    ck, xi, b, rows = block(which, k, d)

                    @pl.loop(0, 2)
                    def _(i):
                        gt = G[ck, xi, :, :, :, pl.ds(pl.multiple_of(i * 256, 256), 256)].reshape(512, 256)
                        cols = pl.ds(pl.multiple_of(b * WIDTH + i * 256, 256), 256)
                        s["H"][rows, :] += dot(gt, s["DOWN"][:, cols], 1, 1)
                        s["C64"][rows, :] += dot(gt, s["L2"][:, cols], 1, 1)

                forward.append(plan.add(fwd, deps=needed(got_x, which, k, d) + [loaded], cost=0.9, rank=10))
                backward.append(plan.add(bwd, deps=needed(got_g, which, k, d) + [loaded2], cost=0.8, rank=20))

    active = []
    for t in range(4):

        def act(t=t):
            rows = slice(t * TILE, t * TILE + TILE)
            mask = s["MK"][rows, 0:64]
            a = (s["A64"][rows, :] * mask).astype(BF)
            gate = s["ACC"][rows, 0:256] + SCALE * dot(a, l1[...])
            s["ACC"][rows, 0:256] = gate
            s["A"][rows, :] = a
            hid = (gate * jax.nn.sigmoid(gate) * s["ACC"][rows, 256:512]).astype(BF)
            s["HID"][rows, :] = hid
            zp = dot(hid, g2t[...], 1, 1) * mask
            s["ZP"][rows, :] = zp
            s["ZS"][rows, :] = (SCALE * zp).astype(BF)

        active.append(plan.add(act, deps=forward + [masked], cost=1.0, rank=11))

    def out_rows(cols, t):
        rows = pl.ds(pl.multiple_of(t * TILE, TILE), TILE)
        o = dot(s["HID"][rows, :], s["DOWN"][:, cols]) + dot(s["ZS"][rows, :], s["L2"][:, cols])
        p = s["PB"][rows, :]
        return o * jnp.concatenate([p, p, p, p], axis=1)

    order_k = (2, 0, 1)
    out_of = {}
    for n, (k, lo) in enumerate([(k, lo) for k in order_k for lo in (0, 1)]):

        def theirs(n=n, k=k, lo=lo):
            b = lo * 6 + halves[1] * 3 + k
            cols = pl.ds(pl.multiple_of(b * WIDTH, WIDTH), WIDTH)

            stage = s["WG" if n < 3 else "WU"].at[n % 3]

            @pl.loop(0, 4)
            def _(t):
                o = out_rows(cols, t).astype(BF)
                for f in (0, 1):
                    half = o[:, f * 256:f * 256 + 256].reshape(2, 8, 16, 256)
                    stage[f, t // 2, pl.ds((t % 2) * 2, 2)] = half

            for f in (0, 1):
                dst = OUT.at[k, pl.ds(lo * 2, 2), :, :, :, pl.ds(f * 256, 256)]
                send(("o", k, lo, f), stage.at[f], dst, sibling)

        plan.add(
            theirs, deps=active + [loaded2], cost=1.6, rank=12 + 0.1 * n,
            sends=[(("o", k, lo, f), "c", 2**19) for f in (0, 1)],
        )

    for n, (k, lo) in enumerate([(k, lo) for k in order_k for lo in (0, 1)]):

        def ours(n=n, k=k, lo=lo):
            b = lo * 6 + halves[0] * 3 + k
            cols = pl.ds(pl.multiple_of(b * WIDTH, WIDTH), WIDTH)

            @pl.loop(0, 4)
            def _(t):
                at = (k, lo * 2 + t // 2, pl.ds((t % 2) * 2, 2))
                o = out_rows(cols, t) + OUT[at].reshape(TILE, WIDTH).astype(F32)
                OUT[at] = o.astype(BF).reshape(2, 8, 16, WIDTH)

        out_of[(k, lo)] = plan.add(ours, deps=active + [("o", k, lo, f) for f in (0, 1)], cost=1.6, rank=12.32 + 0.05 * n)

    def add_block(dst, sources, shape):
        part = shape[0] if len(shape) == 2 else min(4, shape[0])
        for i in range(0, shape[0], part):
            at = pl.ds(i, part)
            total = dst[at].astype(F32)
            for src in sources:
                total = total + src[at].astype(F32)
            dst[at] = total.astype(BF)

    def ring_reduce(name, axis, blk, shape, dep, via, rank):
        me, plus, minus = ring[axis]
        n = SIZE[axis]
        reach = n // 2
        size = 2
        for v in shape:
            size *= v
        chain = {}
        for d in range(reach, 0, -1):
            for sign, to in (("+", plus), ("-", minus)):
                if d == reach and sign != via:
                    continue
                at = around(me, d if sign == "+" else -d, n)
                key = name + (sign, d)
                before = chain.get(sign)

                def run(key=key, at=at, to=to, before=before):
                    if before is not None:
                        add_block(blk(at), [s[before]], shape)
                    send(key, blk(at), s[key], to)

                deps = list(dep) + ([before] if before is not None else [])
                cost = 0.15 if before is None else 0.5
                plan.add(run, deps=deps, rank=rank, cost=cost, sends=[(key, axis + sign, size)])
                chain[sign] = key

        def finish():
            add_block(blk(me), [s[chain[sign]] for sign in "+-"], shape)

        return plan.add(finish, deps=list(dep) + [chain["+"], chain["-"]], cost=0.4, rank=rank)

    def direct_reduce(name, axis, blk, shape, dep, rank):
        me, n = ring[axis][0], SIZE[axis]
        size = 2
        for v in shape:
            size *= v
        keys = []
        for o in sorted(OFFSETS[n][1:], key=lambda o: -abs(o)):
            key = name + (o,)

            def run(key=key, o=o):
                send(key, blk(around(me, o, n)), s[key], at_offset[axis][o])

            link = axis + ("+" if o > 0 else "-")
            plan.add(run, deps=dep(o), rank=rank, cost=0.1, sends=[(key, link, size * abs(o))])
            keys.append(key)

        def finish():
            add_block(blk(me), [s[key] for key in keys], shape)

        return plan.add(finish, deps=dep(0) + keys, cost=0.4, rank=rank)

    def scatter(k):
        axis0, axis1, axis2 = ORDER[k]
        blk0, blk1, sub = views(OUT, k, k)
        ready = [out_of[(k, 0)], out_of[(k, 1)]]
        me1, n1 = ring[axis1][0], SIZE[axis1]
        parts = {}
        for i, r in enumerate(OFFSETS[n1]):
            i1 = around(me1, r, n1)
            parts[r] = ring_reduce(
                ("rs", k, 2, r), axis2, lambda i2, i1=i1: sub(i2, i1), SUB[k], ready, "+-"[i % 2],
                4 - 0.1 * i,
            )
        one = direct_reduce(("rs", k, 1), axis1, blk1, SUB[k], lambda o: [parts[o]], 3)
        return direct_reduce(("rs", k, 0), axis0, blk0, (16, WIDTH), lambda o: [one], 2)

    summed = [scatter(k) for k in order_k]

    reverse = []
    for t in range(4):

        def deact(t=t):
            rows = slice(t * TILE, t * TILE + TILE)
            mask = s["MK"][rows, 0:64]
            cl = (s["C64"][rows, :] * s["MK"][rows, 64:128]).astype(BF)
            s["C"][rows, :] = cl
            p = s["PB"][rows, :]
            dh = s["H"][rows, :] * jnp.concatenate([p, p], axis=1) + SCALE * dot(cl, g2t[...])
            gate = s["ACC"][rows, 0:256]
            sg = jax.nn.sigmoid(gate)
            dg = (dh * s["ACC"][rows, 256:512] * sg * (1.0 + gate * (1.0 - sg))).astype(BF)
            s["DG"][rows, :] = dg
            r = dot(dg, l1[...], 1, 1) * mask
            zr = jnp.concatenate([s["ZP"][rows, :], r], axis=1).T
            z16 = zr[0:16] + zr[16:32] + zr[32:48] + zr[48:64]
            r16 = zr[64:80] + zr[80:96] + zr[96:112] + zr[112:128]
            s["ZR"][t] = jnp.concatenate([z16, r16], axis=0)

        reverse.append(plan.add(deact, deps=backward + active, cost=1.3, rank=21))

    def ex1():
        s["AX"][x] = s["ZR"][x]
        for d in (1, 2, 3):
            send(("e1", d), s["ZR"].at[around(x, d, 4)], s["AX"].at[x], xdev[d])

    def ex2():
        total = s["AX"][0] + s["AX"][1] + s["AX"][2] + s["AX"][3]
        for q in range(4):
            s["YS"][q] = total[q * 8:q * 8 + 8]
        s["AY"][y] = s["YS"][y]
        for d in (1, 2, 3):
            send(("e2", d), s["YS"].at[around(y, d, 4)], s["AY"].at[y], ydev[d])

    def ex3():
        s["HS"][...] = s["AY"][0] + s["AY"][1] + s["AY"][2] + s["AY"][3]
        send(("e3", 1), s["HS"], s["HR"], far)

    def ex4():
        s["FY"][y] = s["HS"][...] + s["HR"][...]
        for d in (1, 2, 3):
            send(("e4", d), s["FY"].at[y], s["FY"].at[y], ydev[d])

    def ex5():
        s["FX"][x] = s["FY"][...]
        for d in (1, 2, 3):
            send(("e5", d), s["FY"], s["FX"].at[x], xdev[d])

    deps = reverse
    for n, (run, axis, size) in enumerate(((ex1, "x", 32768), (ex2, "y", 8192), (ex3, "z", 32768), (ex4, "y", 8192), (ex5, "x", 32768))):
        names = [("e%d" % (n + 1), d) for d in ((1,) if n == 2 else (1, 2, 3))]
        plan.add(run, deps=deps, cost=0.4, rank=0.5, sends=[(m, axis + "+-"[i % 2], size) for i, m in enumerate(names)])
        deps = names

    def lowrank():
        o_gl[...] = (SCALE * dot(s["A"][...], s["DG"][...], 0, 0)).astype(BF)
        o_dd[...] = (SCALE * dot(s["C"][...], s["HID"][...], 0, 0)).astype(BF)

    plan.add(lowrank, deps=reverse, cost=2.0, rank=23)

    def left_sides():
        for t in range(4):
            cols = slice(t * TILE, t * TILE + TILE)
            mt = s["MK"][t * TILE:t * TILE + TILE, :].T
            z16 = s["FX"][t, 0:2].reshape(16, TILE)
            r16 = s["FX"][t, 2:4].reshape(16, TILE)
            s["LZ"][:, cols] = (jnp.concatenate([z16] * 4, axis=0) * mt[64:128]).astype(BF)
            full = jnp.concatenate([r16] * 4, axis=0) * mt[0:64]
            top = full.astype(BF)
            s["LR"][0:64, cols] = top
            s["LR"][64:128, cols] = (full - top.astype(F32)).astype(BF)

    left = plan.add(left_sides, deps=deps, cost=1.5, rank=22)
    for n in range(4):

        def grads(n=n):
            @pl.loop(3 * n, 3 * n + 3)
            def _(b):
                cols = pl.ds(pl.multiple_of(b * WIDTH, WIDTH), WIDTH)
                at = (b % 6, pl.ds((b // 6) * 2, 2))
                o_dl[:, cols] = (SCALE * dot(s["LZ"][...], G[at].reshape(1024, WIDTH))).astype(BF)
                r = dot(s["LR"][...], X[at].reshape(1024, WIDTH))
                o_gd[:, cols] = (SCALE * (r[0:64] + r[64:128])).astype(BF)

        plan.add(grads, deps=[left], cost=2.7, rank=24)

    def give_back():
        for k in range(3):
            done = OUT[k, xp, y, z].astype(F32)
            for q in range(4):
                s["S32"][q, :, k * WIDTH:(k + 1) * WIDTH] = done[q * 4:q * 4 + 4]
        for i, (g, d) in enumerate(mates):
            send(("l", i), s["S32"].at[g], s["MX"].at[grp], d)
        s["MX"][grp] = s["S32"][grp]

    plan.add(give_back, deps=summed, cost=0.5, rank=0, sends=[(("l", i), "c", 24576) for i in range(3)])

    def finish():
        for q in range(4):
            mixed[:, q * 1536:(q + 1) * 1536] = s["MX"][q].astype(BF)

    plan.add(finish, deps=[("l", i) for i in range(3)], cost=0.3, rank=0)

    for i in plan.order():
        task = plan.tasks[i]
        for d in task["deps"]:
            if d in copies and d not in waited:
                copies[d].wait_recv()
                waited.add(d)
        task["run"]()
    for d in copies:
        if d not in waited:
            copies[d].wait_recv()
    for copy in pending:
        copy.wait_send()


def hand_over(*refs):
    for src, dst in zip(refs[:5], refs[5:]):
        dst[...] = src[...]


def local(tokens, out_grad, routes, tasks, route_probs, gate, up, down, g1, l1, g2, l2):
    probs = []
    for j in range(2):
        p = route_probs[:, j]
        hi = lax.reduce_precision(p, 8, 7)
        mid = lax.reduce_precision(p - hi, 8, 7)
        probs += [hi, mid, p - hi - mid]
    fields = [routes[:, 0].astype(F32), routes[:, 1].astype(F32), tasks.astype(F32)] + probs
    meta = jnp.concatenate([f[:, None] for f in fields] + [jnp.zeros((4, 128 - len(fields)), F32)], axis=1)
    shapes = scratch()
    shapes_out = tuple(
        jax.ShapeDtypeStruct(v, BF) for v in ((4, 6144), (64, 6144), (64, 256), (64, 256), (64, 6144))
    )
    w_shape = (3, 2, 2, 4, 8, 16, 256)
    vmem = pl.BlockSpec(memory_space=pltpu.VMEM)
    hbm = pl.BlockSpec(memory_space=pl.ANY)
    mixed, gd, gl, dd, dl = pl.pallas_call(
        functools.partial(body, tuple(shapes)),
        out_shape=shapes_out,
        in_specs=[vmem, vmem, vmem, hbm, hbm, hbm, hbm, vmem, vmem, hbm],
        out_specs=(vmem,) * 5,
        scratch_shapes=list(shapes.values()),
        compiler_params=pltpu.CompilerParams(
            collective_id=0, has_side_effects=True, vmem_limit_bytes=64 * 2**20 - 2**18
        ),
        cost_estimate=pl.CostEstimate(flops=24 * 10**9, bytes_accessed=12 * 10**6, transcendentals=10**6),
    )(tokens, out_grad, meta, gate.reshape(w_shape), up.reshape(w_shape), down[0], g1[0].T, l1[0], g2[0].T, l2[0])
    mixed, gd, gl, dd, dl = pl.pallas_call(
        hand_over, out_shape=shapes_out, in_specs=[vmem] * 5, out_specs=(vmem,) * 5,
    )(mixed, gd, gl, dd, dl)
    return mixed, gd.T[None], gl[None], dd.T[None], dl[None]


def solution(mesh):
    rows = P(("dp", "expert", "tensor"), None)
    return jax.shard_map(
        local,
        mesh=mesh,
        in_specs=(
            rows,
            rows,
            rows,
            P(("dp", "expert", "tensor")),
            rows,
            P("expert", None, ("dp", "tensor")),
            P("expert", None, ("dp", "tensor")),
            P("expert", ("dp", "tensor"), None),
            P("expert", None, None),
            P("expert", None, ("dp", "tensor")),
            P("expert", ("dp", "tensor"), None),
            P("expert", None, None),
        ),
        out_specs=(
            rows,
            P("expert", None, None),
            P("expert", None, ("dp", "tensor")),
            P("expert", ("dp", "tensor"), None),
            P("expert", None, None),
        ),
        check_vma=False,
    )
```

```python
import functools

import jax
import jax.numpy as jnp
import numpy as np
from jax import lax
from jax.experimental import pallas as pl
from jax.experimental.pallas import tpu as pltpu
from jax.sharding import PartitionSpec as P

RANK = 16
SCALE = 0.5
MESH = pl.DeviceIdType.MESH
BF = jnp.bfloat16
F32 = jnp.float32
WIDTH = 512
TILE = 256
MAX_COPIES = 440

ORDER = (("z", "y", "x"), ("z", "x", "y"), ("y", "x", "z"))
SIZE = {"x": 4, "y": 4, "z": 8}
SUB = ((8, 16, WIDTH), (8, 16, WIDTH), (4, 16, WIDTH))
OFFSETS = {4: (0, -1, 1, 2), 8: (0, -1, 1, -2, 2, -3, 3, 4)}


def rs_buffers():
    shapes = {}
    for k in range(3):
        first, second, third = ORDER[k]
        sub = SUB[k]
        reach = SIZE[third] // 2
        for i, r in enumerate(OFFSETS[SIZE[second]]):
            for d in range(1, reach + 1):
                for sign in "+-":
                    if d < reach or sign == "+-"[i % 2]:
                        shapes[("rs", k, 2, r, sign, d)] = pltpu.VMEM(sub, BF)
        for o in OFFSETS[SIZE[second]][1:]:
            shapes[("rs", k, 1, o)] = pltpu.VMEM(sub, BF)
        for o in OFFSETS[SIZE[first]][1:]:
            shapes[("rs", k, 0, o)] = pltpu.VMEM((16, WIDTH), BF)
    return shapes


class Plan:
    RATE = {"x+": 0.046, "x-": 0.046, "y+": 0.046, "y-": 0.046, "z+": 0.04, "z-": 0.04, "c": 0.4}
    DELAY = 2.8

    def __init__(self):
        self.tasks = []

    def add(self, run, deps=(), cost=0.15, rank=5.0, sends=()):
        task = {"run": run, "deps": list(deps), "cost": cost, "rank": rank, "sends": list(sends)}
        self.tasks.append(task)
        return ("task", len(self.tasks) - 1)

    def order(self):
        when, free, now, done = {}, {}, 0.0, []
        left = list(range(len(self.tasks)))
        while left:
            best = None
            for i in left:
                task = self.tasks[i]
                if any(d not in when for d in task["deps"]):
                    continue
                at = max([when[d] for d in task["deps"]] + [0.0])
                key = (max(at, now), task["rank"], i)
                if best is None or key < best[0]:
                    best = (key, i)
            (begin, _, _), i = best
            task = self.tasks[i]
            now = begin + task["cost"]
            when[("task", i)] = now
            for name, link, size in task["sends"]:
                start = max(now, free.get(link, 0.0))
                free[link] = start + size * 1e-6 / self.RATE[link]
                when[name] = free[link] + self.DELAY
            done.append(i)
            left.remove(i)
        self.length = now
        return done


def scratch():
    shapes = {
        "X": pltpu.VMEM((6, 4, 4, 8, 16, WIDTH), BF),
        "G": pltpu.VMEM((6, 4, 4, 8, 16, WIDTH), BF),
        "OUT": pltpu.VMEM((3, 4, 4, 8, 16, WIDTH), BF),
        "DOWN": pltpu.VMEM((256, 6144), BF),
        "WG": pltpu.VMEM((3, 2, 2, 4, 8, 16, 256), BF),
        "WU": pltpu.VMEM((3, 2, 2, 4, 8, 16, 256), BF),
        "G1T": pltpu.VMEM((64, 6144), BF),
        "L2": pltpu.VMEM((64, 6144), BF),
        "ACC": pltpu.VMEM((1024, 512), F32),
        "A64": pltpu.VMEM((1024, 64), F32),
        "C64": pltpu.VMEM((1024, 64), F32),
        "H": pltpu.VMEM((1024, 256), F32),
        "MK": pltpu.VMEM((1024, 128), F32),
        "PB": pltpu.VMEM((1024, 128), F32),
        "ZP": pltpu.VMEM((1024, 64), F32),
        "HID": pltpu.VMEM((1024, 256), BF),
        "DG": pltpu.VMEM((1024, 256), BF),
        "A": pltpu.VMEM((1024, 64), BF),
        "ZS": pltpu.VMEM((1024, 64), BF),
        "C": pltpu.VMEM((1024, 64), BF),
        "T32": pltpu.VMEM((2, 4, 4, 1536), F32),
        "M32": pltpu.VMEM((4, 128), F32),
        "R": pltpu.VMEM((2, 4, 4, 1536), F32),
        "MR": pltpu.VMEM((4, 4, 128), F32),
        "F": pltpu.VMEM((2, 16, 1536), F32),
        "FM": pltpu.VMEM((16, 128), F32),
        "MZ": pltpu.VMEM((8, 16, 128), BF),
        "MF": pltpu.VMEM((2, 4, 16, 128), BF),
        "ZR": pltpu.VMEM((4, 32, 256), F32),
        "AX": pltpu.VMEM((4, 32, 256), F32),
        "YS": pltpu.VMEM((4, 8, 256), F32),
        "AY": pltpu.VMEM((4, 8, 256), F32),
        "HS": pltpu.VMEM((8, 256), F32),
        "HR": pltpu.VMEM((8, 256), F32),
        "FY": pltpu.VMEM((4, 8, 256), F32),
        "FX": pltpu.VMEM((4, 4, 8, 256), F32),
        "LZ": pltpu.VMEM((64, 1024), BF),
        "LR": pltpu.VMEM((128, 1024), BF),
        "S32": pltpu.VMEM((4, 4, 1536), F32),
        "MX": pltpu.VMEM((4, 4, 1536), F32),
        "send": pltpu.SemaphoreType.DMA((MAX_COPIES,)),
        "recv": pltpu.SemaphoreType.DMA((MAX_COPIES,)),
        "local": pltpu.SemaphoreType.DMA((8,)),
    }
    shapes.update(rs_buffers())
    return shapes


def dot(a, b, ca=1, cb=0):
    return lax.dot_general(a, b, (((ca,), (cb,)), ((), ())), preferred_element_type=F32)


def body(names, tok, og, meta, wg, wu, down, g1t, l1, g2t, l2, mixed, o_gd, o_gl, o_dd, o_dl, *refs):
    s = dict(zip(names, refs))
    X, G, OUT = s["X"], s["G"], s["OUT"]
    dp, ex, x = lax.axis_index("dp"), lax.axis_index("expert"), lax.axis_index("tensor")
    h, y = dp // 4, dp % 4
    zl, c = ex // 2, ex % 2
    z = h * 4 + zl
    xlo, xhi = x % 2, x // 2
    xp = xlo * 2 + xhi
    grp = xlo * 2 + c

    def device(x_, y_, z_, c_):
        return ((z_ // 4) * 4 + y_, (z_ % 4) * 2 + c_, x_)

    def around(v, d, n):
        return lax.rem(v + (d + n), n)

    def xperm(i):
        return lax.rem(i, 2) * 2 + i // 2

    xdev = [device(around(x, d, 4), y, z, c) for d in range(4)]
    ydev = [device(x, around(y, d, 4), z, c) for d in range(4)]
    zdev = {1: device(x, y, around(z, 1, 8), c), -1: device(x, y, around(z, -1, 8), c)}
    far = device(x, y, around(z, 4, 8), c)
    sibling = device(x, y, z, 1 - c)
    xpair = xhi * 2 + (1 - xlo)
    pair = device(xpair, y, z, c)
    pair_sibling = device(xpair, y, z, 1 - c)
    ring = {"x": (x, xdev[1], xdev[3]), "y": (y, ydev[1], ydev[3]), "z": (z, zdev[1], zdev[-1])}
    at_offset = {
        "x": {o: xdev[o % 4] for o in OFFSETS[4]},
        "y": {o: ydev[o % 4] for o in OFFSETS[4]},
        "z": {o: device(x, y, around(z, o, 8), c) for o in OFFSETS[8]},
    }
    plan = Plan()
    copies, waited, pending = {}, set(), []

    def send(name, src, dst, target):
        i = len(copies)
        copy = pltpu.make_async_remote_copy(
            src_ref=src, dst_ref=dst, send_sem=s["send"].at[i], recv_sem=s["recv"].at[i],
            device_id=target, device_id_type=MESH,
        )
        copy.start()
        copies[name] = copy
        pending.append(copy)

    local_down = pltpu.make_async_copy(down, s["DOWN"], s["local"].at[0])
    local_g1 = pltpu.make_async_copy(g1t, s["G1T"], s["local"].at[1])
    local_l2 = pltpu.make_async_copy(l2, s["L2"], s["local"].at[2])

    local_wg = pltpu.make_async_copy(wg, s["WG"], s["local"].at[3])
    local_wu = pltpu.make_async_copy(wu, s["WU"], s["local"].at[4])

    barrier = pltpu.get_barrier_semaphore()
    greeted = xdev[1:] + ydev[1:] + [at_offset["z"][o] for o in OFFSETS[8][1:]] + [sibling, pair_sibling]
    for target in greeted:
        pl.semaphore_signal(barrier, inc=1, device_id=target, device_id_type=MESH)
    local_down.start()
    local_g1.start()
    local_l2.start()
    local_wg.start()
    local_wu.start()
    for q in range(4):
        s["T32"][0, q] = tok[:, q * 1536:(q + 1) * 1536].astype(F32)
        s["T32"][1, q] = og[:, q * 1536:(q + 1) * 1536].astype(F32)
    s["M32"][...] = meta[...].astype(F32)
    pl.semaphore_wait(barrier, len(greeted))

    mates = ((xlo * 2 + 1 - c, sibling), ((1 - xlo) * 2 + c, pair), ((1 - xlo) * 2 + 1 - c, pair_sibling))
    for name, src, dst in (("t0", "T32", "R"), ("m", "M32", "MR"), ("t1", "T32", "R")):
        for i, (g, d) in enumerate(mates):
            if name == "m":
                send((name, i), s["M32"], s["MR"].at[grp], d)
            else:
                a = int(name[1])
                send((name, i), s["T32"].at[a, g], s["R"].at[a, grp], d)
    s["R"][0, grp] = s["T32"][0, grp]
    s["R"][1, grp] = s["T32"][1, grp]
    s["MR"][grp] = s["M32"][...]
    s["ACC"][...] = jnp.zeros((1024, 512), F32)
    s["A64"][...] = jnp.zeros((1024, 64), F32)
    s["C64"][...] = jnp.zeros((1024, 64), F32)
    s["H"][...] = jnp.zeros((1024, 256), F32)
    arrived_first = plan.add(lambda: None, cost=0.0, sends=[((n, i), "c", 1000) for n in ("t0", "m", "t1") for i in range(3)])

    def own_block(a, buf):
        def run():
            for q in range(4):
                s["F"][a, q * 4:q * 4 + 4, :] = s["R"][a, q]
            for k in range(3):
                buf[c * 3 + k, xp, y, z] = s["F"][a, :, k * WIDTH:(k + 1) * WIDTH].astype(BF)

        return plan.add(run, deps=[("t%d" % a, i) for i in range(3)], cost=0.5, rank=1)

    def views(buf, lead, k):
        if k == 0:
            return (
                lambda i: buf.at[lead, xp, y, i],
                lambda i: buf.at[lead, xp, i],
                lambda i2, i1: buf.at[lead, xperm(i2), i1],
            )
        if k == 1:
            return (
                lambda i: buf.at[lead, xp, y, i],
                lambda i: buf.at[lead, xperm(i), y],
                lambda i2, i1: buf.at[lead, xperm(i1), i2],
            )
        return (
            lambda i: buf.at[lead, xp, i, z],
            lambda i: buf.at[lead, xperm(i), :, z],
            lambda i2, i1: buf.at[lead, xperm(i1), :, i2],
        )

    def ring_gather(name, axis, blk, size, dep, via, rank):
        me, plus, minus = ring[axis]
        n = SIZE[axis]
        reach = n // 2
        have = {0: list(dep)}
        for d in range(reach):
            for sign, to in (("+", plus), ("-", minus)):
                if d == reach - 1 and via != sign:
                    continue
                mine = around(me, -d if sign == "+" else d, n)
                deps = dep if d == 0 else [name + (sign, d)]
                key = name + (sign, d + 1)

                def run(key=key, mine=mine, to=to):
                    send(key, blk(mine), blk(mine), to)

                plan.add(run, deps=deps, cost=0.15, rank=rank, sends=[(key, axis + sign, size)])
                have[reach if d == reach - 1 else (-(d + 1) if sign == "+" else d + 1)] = [key]
        return have

    def direct_gather(name, axis, blk, size, dep, rank):
        me, n = ring[axis][0], SIZE[axis]
        have = {0: list(dep)}
        for o in OFFSETS[n][1:]:
            key = name + (o,)

            def run(key=key, o=o):
                send(key, blk(me), blk(me), at_offset[axis][o])

            link = axis + ("+" if o > 0 else "-")
            plan.add(run, deps=dep, cost=0.15, rank=rank, sends=[(key, link, size * abs(o))])
            have[o if 2 * o == n else -o] = [key]
        return have

    def gather(a, buf, k, dep, gate1, gate2, rank):
        ck = c * 3 + k
        axis0, axis1, axis2 = ORDER[k]
        blk0, blk1, sub = views(buf, ck, k)
        piece = 16 * WIDTH * 2
        have0 = direct_gather((a, k, 0), axis0, blk0, piece, dep + gate1, rank)
        dep1 = [d for v in have0.values() for d in v]
        size1 = piece * SIZE[axis0]
        have1 = direct_gather((a, k, 1), axis1, blk1, size1, dep1, rank)
        own, other = {}, {}
        me1, me2, n1, n2 = ring[axis1][0], ring[axis2][0], SIZE[axis1], SIZE[axis2]
        for i, r in enumerate(OFFSETS[n1]):
            i1 = around(me1, r, n1)
            have2 = ring_gather(
                (a, k, 2, r), axis2, lambda i2, i1=i1: sub(i2, i1), size1, have1[r] + gate2, "+-"[i % 2],
                rank + 0.01 * i,
            )
            for o, deps in have2.items():
                own[(r, o)] = deps
        for o in OFFSETS[n2]:
            key = ("f", a, k, o)

            def run(key=key, o=o):
                i2 = around(me2, o, n2)
                ref = buf.at[ck, xperm(i2)] if k == 0 else buf.at[ck, :, i2] if k == 1 else buf.at[ck, :, :, i2]
                send(key, ref, ref, sibling)

            deps = [d for r in OFFSETS[n1] for d in own[(r, o)]]
            plan.add(run, deps=deps, cost=0.15, rank=rank + 0.5, sends=[(key, "c", size1 * 4)])
            for r in OFFSETS[n1]:
                other[(r, o)] = [key]
        return own, other

    own_x, own_g = own_block(0, X), own_block(1, G)
    got_x = [gather("x", X, k, [own_x], [], [], 1) for k in range(3)]
    gates = []
    for k in range(3):
        near = [got_x[k][0][(r, o)] for r in OFFSETS[SIZE[ORDER[k][1]]] for o in (-1, 1)]
        gates.append([d for v in near for d in v])
    got_g = [
        gather("g", G, k, [own_g], [], gates[k], 2) for k in range(3)
    ]

    def meta_own():
        for q in range(4):
            s["FM"][q * 4:q * 4 + 4, :] = s["MR"][q]
        s["MZ"][z] = pltpu.roll(s["FM"][...], z * 16, 1).astype(BF)

    def meta_sum():
        total = s["MZ"][0].astype(F32)
        for i in range(1, 8):
            total = total + s["MZ"][i].astype(F32)
        s["MF"][xhi, y] = total.astype(BF)

    t = plan.add(meta_own, deps=[("m", i) for i in range(3)], cost=0.3, rank=3)
    have = direct_gather(("mz",), "z", lambda i: s["MZ"].at[i], 4096, [t], 3)
    t = plan.add(meta_sum, deps=[d for v in have.values() for d in v], cost=0.3, rank=3)
    have = direct_gather(("my",), "y", lambda i: s["MF"].at[xhi, i], 4096, [t], 3)
    t = plan.add(
        lambda: send("mx", s["MF"].at[xhi], s["MF"].at[xhi], xdev[2]),
        deps=[d for v in have.values() for d in v], rank=3, sends=[("mx", "x+", 16384)],
    )

    def masks():
        fields = s["MF"][...].astype(F32).reshape(128, 128)
        me_f = ex.astype(F32)
        band = (lax.broadcasted_iota(jnp.int32, (128, 64), 1) // RANK).astype(F32)
        for i in range(8):
            f = fields if i == 0 else pltpu.roll(fields, 128 - 16 * i, 1)
            hit0 = jnp.where(f[:, 0:1] == me_f, 1.0, 0.0)
            hit1 = jnp.where(f[:, 1:2] == me_f, 1.0, 0.0)
            p0 = f[:, 3:4] + f[:, 4:5] + f[:, 5:6]
            p1 = f[:, 6:7] + f[:, 7:8] + f[:, 8:9]
            p = hit0 * p0 + hit1 * p1
            mask = jnp.where(f[:, 2:3] == band, 1.0, 0.0) * (hit0 + hit1)
            both = jnp.concatenate([mask, mask * p], axis=1)
            wide = jnp.broadcast_to(p, (128, 128))
            for g in range(8):
                rows = slice((g * 8 + i) * 16, (g * 8 + i) * 16 + 16)
                s["MK"][rows, :] = both[g * 16:g * 16 + 16, :]
                s["PB"][rows, :] = wide[g * 16:g * 16 + 16, :]

    masked = plan.add(masks, deps=["mx", t], cost=2.0, rank=6)

    loaded = plan.add(lambda: [copy.wait() for copy in (local_wg, local_wu, local_g1)], cost=0.1, rank=7)
    loaded2 = plan.add(lambda: [copy.wait() for copy in (local_down, local_l2)], cost=0.1, rank=7)
    halves = (c, 1 - c)

    def needed(got, which, k, d):
        found = got[k][which]
        if k == 0:
            keys = [found[(r, d)] for r in OFFSETS[4]]
        else:
            keys = [found[(d, o)] for o in OFFSETS[SIZE[ORDER[k][2]]]]
        return [dep for v in keys for dep in v]

    def block(which, k, d):
        at = around(x, d, 4)
        ck = halves[which] * 3 + k
        rows = pl.ds(pl.multiple_of((at // 2) * 512, 512), 512)
        return ck, xperm(at), lax.rem(at, 2) * 6 + ck, rows

    forward, backward = [], []
    for k in range(3):
        for which in (0, 1):
            for d in OFFSETS[4]:

                def fwd(k=k, which=which, d=d):
                    ck, xi, b, rows = block(which, k, d)

                    @pl.loop(0, 2)
                    def _(i):
                        xt = X[ck, xi, :, :, :, pl.ds(pl.multiple_of(i * 256, 256), 256)].reshape(512, 256)
                        at = (b // 4, (b // 2) % 2, b % 2, pl.ds(i * 2, 2))
                        s["ACC"][rows, 0:256] += dot(xt, s["WG"][at].reshape(256, 256))
                        s["ACC"][rows, 256:512] += dot(xt, s["WU"][at].reshape(256, 256))
                        cols = pl.ds(pl.multiple_of(b * WIDTH + i * 256, 256), 256)
                        s["A64"][rows, :] += dot(xt, s["G1T"][:, cols], 1, 1)

                def bwd(k=k, which=which, d=d):
                    ck, xi, b, rows = block(which, k, d)

                    @pl.loop(0, 2)
                    def _(i):
                        gt = G[ck, xi, :, :, :, pl.ds(pl.multiple_of(i * 256, 256), 256)].reshape(512, 256)
                        cols = pl.ds(pl.multiple_of(b * WIDTH + i * 256, 256), 256)
                        s["H"][rows, :] += dot(gt, s["DOWN"][:, cols], 1, 1)
                        s["C64"][rows, :] += dot(gt, s["L2"][:, cols], 1, 1)

                forward.append(plan.add(fwd, deps=needed(got_x, which, k, d) + [loaded], cost=0.7, rank=10))
                backward.append(plan.add(bwd, deps=needed(got_g, which, k, d) + [loaded2], cost=0.6, rank=20))

    active = []
    for t in range(4):

        def act(t=t):
            rows = slice(t * TILE, t * TILE + TILE)
            mask = s["MK"][rows, 0:64]
            a = (s["A64"][rows, :] * mask).astype(BF)
            gate = s["ACC"][rows, 0:256] + SCALE * dot(a, l1[...])
            s["ACC"][rows, 0:256] = gate
            s["A"][rows, :] = a
            hid = (gate * jax.nn.sigmoid(gate) * s["ACC"][rows, 256:512]).astype(BF)
            s["HID"][rows, :] = hid
            zp = dot(hid, g2t[...], 1, 1) * mask
            s["ZP"][rows, :] = zp
            s["ZS"][rows, :] = (SCALE * zp).astype(BF)

        active.append(plan.add(act, deps=forward + [masked], cost=1.0, rank=11))

    def out_rows(cols, t):
        rows = pl.ds(pl.multiple_of(t * TILE, TILE), TILE)
        o = dot(s["HID"][rows, :], s["DOWN"][:, cols]) + dot(s["ZS"][rows, :], s["L2"][:, cols])
        p = s["PB"][rows, :]
        return o * jnp.concatenate([p, p, p, p], axis=1)

    order_k = (2, 0, 1)
    out_of = {}
    for n, (k, lo) in enumerate([(k, lo) for k in order_k for lo in (0, 1)]):

        def theirs(n=n, k=k, lo=lo):
            b = lo * 6 + halves[1] * 3 + k
            cols = pl.ds(pl.multiple_of(b * WIDTH, WIDTH), WIDTH)

            stage = s["WG" if n < 3 else "WU"].at[n % 3]

            @pl.loop(0, 4)
            def _(t):
                o = out_rows(cols, t).astype(BF)
                for f in (0, 1):
                    half = o[:, f * 256:f * 256 + 256].reshape(2, 8, 16, 256)
                    stage[f, t // 2, pl.ds((t % 2) * 2, 2)] = half

            for f in (0, 1):
                dst = OUT.at[k, pl.ds(lo * 2, 2), :, :, :, pl.ds(f * 256, 256)]
                send(("o", k, lo, f), stage.at[f], dst, sibling)

        plan.add(
            theirs, deps=active + [loaded2], cost=1.6, rank=12 + 0.1 * n,
            sends=[(("o", k, lo, f), "c", 2**19) for f in (0, 1)],
        )

    for n, (k, lo) in enumerate([(k, lo) for k in order_k for lo in (0, 1)]):

        def ours(n=n, k=k, lo=lo):
            b = lo * 6 + halves[0] * 3 + k
            cols = pl.ds(pl.multiple_of(b * WIDTH, WIDTH), WIDTH)

            @pl.loop(0, 4)
            def _(t):
                at = (k, lo * 2 + t // 2, pl.ds((t % 2) * 2, 2))
                o = out_rows(cols, t) + OUT[at].reshape(TILE, WIDTH).astype(F32)
                OUT[at] = o.astype(BF).reshape(2, 8, 16, WIDTH)

        out_of[(k, lo)] = plan.add(ours, deps=active + [("o", k, lo, f) for f in (0, 1)], cost=1.6, rank=12.32 + 0.05 * n)

    def add_block(dst, sources, shape):
        part = shape[0] if len(shape) == 2 else min(4, shape[0])
        for i in range(0, shape[0], part):
            at = pl.ds(i, part)
            total = dst[at].astype(F32)
            for src in sources:
                total = total + src[at].astype(F32)
            dst[at] = total.astype(BF)

    def ring_reduce(name, axis, blk, shape, dep, via, rank):
        me, plus, minus = ring[axis]
        n = SIZE[axis]
        reach = n // 2
        size = 2
        for v in shape:
            size *= v
        chain = {}
        for d in range(reach, 0, -1):
            for sign, to in (("+", plus), ("-", minus)):
                if d == reach and sign != via:
                    continue
                at = around(me, d if sign == "+" else -d, n)
                key = name + (sign, d)
                before = chain.get(sign)

                def run(key=key, at=at, to=to, before=before):
                    if before is not None:
                        add_block(blk(at), [s[before]], shape)
                    send(key, blk(at), s[key], to)

                deps = list(dep) + ([before] if before is not None else [])
                cost = 0.15 if before is None else 0.5
                plan.add(run, deps=deps, rank=rank, cost=cost, sends=[(key, axis + sign, size)])
                chain[sign] = key

        def finish():
            add_block(blk(me), [s[chain[sign]] for sign in "+-"], shape)

        return plan.add(finish, deps=list(dep) + [chain["+"], chain["-"]], cost=0.4, rank=rank)

    def direct_reduce(name, axis, blk, shape, dep, rank):
        me, n = ring[axis][0], SIZE[axis]
        size = 2
        for v in shape:
            size *= v
        keys = []
        for o in sorted(OFFSETS[n][1:], key=lambda o: -abs(o)):
            key = name + (o,)

            def run(key=key, o=o):
                send(key, blk(around(me, o, n)), s[key], at_offset[axis][o])

            link = axis + ("+" if o > 0 else "-")
            plan.add(run, deps=dep(o), rank=rank, cost=0.1, sends=[(key, link, size * abs(o))])
            keys.append(key)

        def finish():
            add_block(blk(me), [s[key] for key in keys], shape)

        return plan.add(finish, deps=dep(0) + keys, cost=0.4, rank=rank)

    def scatter(k):
        axis0, axis1, axis2 = ORDER[k]
        blk0, blk1, sub = views(OUT, k, k)
        ready = [out_of[(k, 0)], out_of[(k, 1)]]
        me1, n1 = ring[axis1][0], SIZE[axis1]
        parts = {}
        for i, r in enumerate(OFFSETS[n1]):
            i1 = around(me1, r, n1)
            parts[r] = ring_reduce(
                ("rs", k, 2, r), axis2, lambda i2, i1=i1: sub(i2, i1), SUB[k], ready, "+-"[i % 2],
                4 - 0.1 * i,
            )
        one = direct_reduce(("rs", k, 1), axis1, blk1, SUB[k], lambda o: [parts[o]], 3)
        return direct_reduce(("rs", k, 0), axis0, blk0, (16, WIDTH), lambda o: [one], 2)

    summed = [scatter(k) for k in order_k]

    reverse = []
    for t in range(4):

        def deact(t=t):
            rows = slice(t * TILE, t * TILE + TILE)
            mask = s["MK"][rows, 0:64]
            cl = (s["C64"][rows, :] * s["MK"][rows, 64:128]).astype(BF)
            s["C"][rows, :] = cl
            p = s["PB"][rows, :]
            dh = s["H"][rows, :] * jnp.concatenate([p, p], axis=1) + SCALE * dot(cl, g2t[...])
            gate = s["ACC"][rows, 0:256]
            sg = jax.nn.sigmoid(gate)
            dg = (dh * s["ACC"][rows, 256:512] * sg * (1.0 + gate * (1.0 - sg))).astype(BF)
            s["DG"][rows, :] = dg
            r = dot(dg, l1[...], 1, 1) * mask
            zr = jnp.concatenate([s["ZP"][rows, :], r], axis=1).T
            z16 = zr[0:16] + zr[16:32] + zr[32:48] + zr[48:64]
            r16 = zr[64:80] + zr[80:96] + zr[96:112] + zr[112:128]
            s["ZR"][t] = jnp.concatenate([z16, r16], axis=0)

        reverse.append(plan.add(deact, deps=backward + active, cost=1.3, rank=21))

    def ex1():
        s["AX"][x] = s["ZR"][x]
        for d in (1, 2, 3):
            send(("e1", d), s["ZR"].at[around(x, d, 4)], s["AX"].at[x], xdev[d])

    def ex2():
        total = s["AX"][0] + s["AX"][1] + s["AX"][2] + s["AX"][3]
        for q in range(4):
            s["YS"][q] = total[q * 8:q * 8 + 8]
        s["AY"][y] = s["YS"][y]
        for d in (1, 2, 3):
            send(("e2", d), s["YS"].at[around(y, d, 4)], s["AY"].at[y], ydev[d])

    def ex3():
        s["HS"][...] = s["AY"][0] + s["AY"][1] + s["AY"][2] + s["AY"][3]
        send(("e3", 1), s["HS"], s["HR"], far)

    def ex4():
        s["FY"][y] = s["HS"][...] + s["HR"][...]
        for d in (1, 2, 3):
            send(("e4", d), s["FY"].at[y], s["FY"].at[y], ydev[d])

    def ex5():
        s["FX"][x] = s["FY"][...]
        for d in (1, 2, 3):
            send(("e5", d), s["FY"], s["FX"].at[x], xdev[d])

    deps = reverse
    for n, (run, axis, size) in enumerate(((ex1, "x", 32768), (ex2, "y", 8192), (ex3, "z", 32768), (ex4, "y", 8192), (ex5, "x", 32768))):
        names = [("e%d" % (n + 1), d) for d in ((1,) if n == 2 else (1, 2, 3))]
        plan.add(run, deps=deps, cost=0.4, rank=0.5, sends=[(m, axis + "+-"[i % 2], size) for i, m in enumerate(names)])
        deps = names

    def lowrank():
        o_gl[...] = (SCALE * dot(s["A"][...], s["DG"][...], 0, 0)).astype(BF)
        o_dd[...] = (SCALE * dot(s["C"][...], s["HID"][...], 0, 0)).astype(BF)

    plan.add(lowrank, deps=reverse, cost=2.0, rank=23)

    def left_sides():
        for t in range(4):
            cols = slice(t * TILE, t * TILE + TILE)
            mt = s["MK"][t * TILE:t * TILE + TILE, :].T
            z16 = s["FX"][t, 0:2].reshape(16, TILE)
            r16 = s["FX"][t, 2:4].reshape(16, TILE)
            s["LZ"][:, cols] = (jnp.concatenate([z16] * 4, axis=0) * mt[64:128]).astype(BF)
            full = jnp.concatenate([r16] * 4, axis=0) * mt[0:64]
            top = full.astype(BF)
            s["LR"][0:64, cols] = top
            s["LR"][64:128, cols] = (full - top.astype(F32)).astype(BF)

    left = plan.add(left_sides, deps=deps, cost=1.5, rank=22)
    for n in range(4):

        def grads(n=n):
            @pl.loop(3 * n, 3 * n + 3)
            def _(b):
                cols = pl.ds(pl.multiple_of(b * WIDTH, WIDTH), WIDTH)
                at = (b % 6, pl.ds((b // 6) * 2, 2))
                o_dl[:, cols] = (SCALE * dot(s["LZ"][...], G[at].reshape(1024, WIDTH))).astype(BF)
                r = dot(s["LR"][...], X[at].reshape(1024, WIDTH))
                o_gd[:, cols] = (SCALE * (r[0:64] + r[64:128])).astype(BF)

        plan.add(grads, deps=[left], cost=2.7, rank=24)

    def give_back():
        for k in range(3):
            done = OUT[k, xp, y, z].astype(F32)
            for q in range(4):
                s["S32"][q, :, k * WIDTH:(k + 1) * WIDTH] = done[q * 4:q * 4 + 4]
        for i, (g, d) in enumerate(mates):
            send(("l", i), s["S32"].at[g], s["MX"].at[grp], d)
        s["MX"][grp] = s["S32"][grp]

    plan.add(give_back, deps=summed, cost=0.5, rank=0, sends=[(("l", i), "c", 24576) for i in range(3)])

    def finish():
        for q in range(4):
            mixed[:, q * 1536:(q + 1) * 1536] = s["MX"][q].astype(BF)

    plan.add(finish, deps=[("l", i) for i in range(3)], cost=0.3, rank=0)

    for i in plan.order():
        task = plan.tasks[i]
        for d in task["deps"]:
            if d in copies and d not in waited:
                copies[d].wait_recv()
                waited.add(d)
        task["run"]()
    for d in copies:
        if d not in waited:
            copies[d].wait_recv()
    for copy in pending:
        copy.wait_send()


def hand_over(*refs):
    for src, dst in zip(refs[:5], refs[5:]):
        dst[...] = src[...]


def local(tokens, out_grad, routes, tasks, route_probs, gate, up, down, g1, l1, g2, l2):
    probs = []
    for j in range(2):
        p = route_probs[:, j]
        hi = lax.reduce_precision(p, 8, 7)
        mid = lax.reduce_precision(p - hi, 8, 7)
        probs += [hi, mid, p - hi - mid]
    fields = [routes[:, 0].astype(F32), routes[:, 1].astype(F32), tasks.astype(F32)] + probs
    lanes = np.eye(len(fields), 128, dtype=np.float32)
    meta = sum(f[:, None] * lanes[i][None, :] for i, f in enumerate(fields))
    shapes = scratch()
    shapes_out = tuple(
        jax.ShapeDtypeStruct(v, BF) for v in ((4, 6144), (64, 6144), (64, 256), (64, 256), (64, 6144))
    )
    w_shape = (3, 2, 2, 4, 8, 16, 256)
    vmem = pl.BlockSpec(memory_space=pltpu.VMEM)
    hbm = pl.BlockSpec(memory_space=pl.ANY)
    mixed, gd, gl, dd, dl = pl.pallas_call(
        functools.partial(body, tuple(shapes)),
        out_shape=shapes_out,
        in_specs=[vmem, vmem, vmem, hbm, hbm, hbm, hbm, vmem, vmem, hbm],
        out_specs=(vmem,) * 5,
        scratch_shapes=list(shapes.values()),
        compiler_params=pltpu.CompilerParams(
            collective_id=0, has_side_effects=True, vmem_limit_bytes=64 * 2**20 - 2**18
        ),
        cost_estimate=pl.CostEstimate(flops=24 * 10**9, bytes_accessed=12 * 10**6, transcendentals=10**6),
    )(tokens, out_grad, meta, gate.reshape(w_shape), up.reshape(w_shape), down[0], g1[0].T, l1[0], g2[0].T, l2[0])
    mixed, gd, gl, dd, dl = pl.pallas_call(
        hand_over, out_shape=shapes_out, in_specs=[vmem] * 5, out_specs=(vmem,) * 5,
    )(mixed, gd, gl, dd, dl)
    return mixed, gd.T[None], gl[None], dd.T[None], dl[None]


def solution(mesh):
    rows = P(("dp", "expert", "tensor"), None)
    return jax.shard_map(
        local,
        mesh=mesh,
        in_specs=(
            rows,
            rows,
            rows,
            P(("dp", "expert", "tensor")),
            rows,
            P("expert", None, ("dp", "tensor")),
            P("expert", None, ("dp", "tensor")),
            P("expert", ("dp", "tensor"), None),
            P("expert", None, None),
            P("expert", None, ("dp", "tensor")),
            P("expert", ("dp", "tensor"), None),
            P("expert", None, None),
        ),
        out_specs=(
            rows,
            P("expert", None, None),
            P("expert", None, ("dp", "tensor")),
            P("expert", ("dp", "tensor"), None),
            P("expert", None, None),
        ),
        check_vma=False,
    )
```
